32 devices in a mesh: expert: 8 (over z, y), head: 4 (over x, core).
Axes of the slice: x: 2, y: 2, z: 4, core: 2. Of those that a mesh axis runs over, the one named last changes fastest.
Arguments:
- block_input: bfloat16 [25216, 384], P(('expert', 'head')), may hold values from -6 to 6
- out_cotangent: bfloat16 [25216, 384], P(('expert', 'head')), may hold values from -6 to 6
- route_ids: int32 [25216, 2], P(('expert', 'head')), may hold values from 0 to 7, all different within a row; in each aligned block of 788 rows (0 to 787, 788 to 1575, ...) at most 590 rows name the same one
- capacity: int32 [8], replicated, may hold values from 148 to 295, as said below
- qkv_weight: float32 [384, 1152], P('head'), may hold values from -0.375 to 0.375
- qkv_first: float32 [384, 1152], P('head'), may hold values from -56 to 56
- qkv_second: float32 [384, 1152], P('head'), may hold values from 6.304 to 25.216
- proj_weight: float32 [384, 384], P('head'), may hold values from -1.25 to 1.25
- proj_first: float32 [384, 384], P('head'), may hold values from -28 to 28
- proj_second: float32 [384, 384], P('head'), may hold values from 1.576 to 6.304
- router_weight: float32 [384, 8], P('head'), may hold values from -0.25 to 0.25
- router_first: float32 [384, 8], P('head'), may hold values from -224 to 224
- router_second: float32 [384, 8], P('head'), may hold values from 100.864 to 403.456
- norm_params: float32 [384, 4], P('head'), may hold values from -2 to 2.5
- norm_first: float32 [384, 4], P('head'), may hold values from -56 to 56
- norm_second: float32 [384, 4], P('head'), may hold values from 6.304 to 25.216
- expert_up: float32 [8, 384, 1536], P('expert', None, 'head'), may hold values from -0.3125 to 0.3125
- up_first: float32 [8, 384, 1536], P('expert', None, 'head'), may hold values from -8 to 8
- up_second: float32 [8, 384, 1536], P('expert', None, 'head'), may hold values from 0.14184 to 0.56736
- expert_down: float32 [8, 384, 1536], P('expert', None, 'head'), may hold values from -0.15309311 to 0.15309311
- down_first: float32 [8, 384, 1536], P('expert', None, 'head'), may hold values from -16 to 16
- down_second: float32 [8, 384, 1536], P('expert', None, 'head'), may hold values from 0.56736 to 2.26944
Outputs:
- block_output: bfloat16 [25216, 384], P(('expert', 'head'))
- input_grad: bfloat16 [25216, 384], P(('expert', 'head'))
- qkv_new: float32 [384, 1152], P('head')
- qkv_copy: bfloat16 [384, 1152], P('head')
- qkv_first_new: float32 [384, 1152], P('head')
- qkv_second_new: float32 [384, 1152], P('head')
- proj_new: float32 [384, 384], P('head')
- proj_copy: bfloat16 [384, 384], P('head')
- proj_first_new: float32 [384, 384], P('head')
- proj_second_new: float32 [384, 384], P('head')
- router_new: float32 [384, 8], P('head')
- router_copy: bfloat16 [384, 8], P('head')
- router_first_new: float32 [384, 8], P('head')
- router_second_new: float32 [384, 8], P('head')
- norm_new: float32 [384, 4], P('head')
- norm_copy: bfloat16 [384, 4], P('head')
- norm_first_new: float32 [384, 4], P('head')
- norm_second_new: float32 [384, 4], P('head')
- up_new: float32 [8, 384, 1536], P('expert', None, 'head')
- up_copy: bfloat16 [8, 384, 1536], P('expert', None, 'head')
- up_first_new: float32 [8, 384, 1536], P('expert', None, 'head')
- up_second_new: float32 [8, 384, 1536], P('expert', None, 'head')
- down_new: float32 [8, 384, 1536], P('expert', None, 'head')
- down_copy: bfloat16 [8, 384, 1536], P('expert', None, 'head')
- down_first_new: float32 [8, 384, 1536], P('expert', None, 'head')
- down_second_new: float32 [8, 384, 1536], P('expert', None, 'head')
- dense_norms: float32 [7, 2], replicated
- expert_norms: float32 [8, 4], P('expert')
The draws below stay inside these ranges and needn't reach their ends.
Inputs may be any that keep to these rules, and one draw needn't show every extreme that they name: `route_ids`: A token's two experts differ; in the 788 rows of one device no expert is named more than 2 * 295 times. One expert's capacity is exactly 295.
All inputs are finite; a program needn't handle non-finite values.
Results may differ from the reference program's by a relative error of at most 0.015.
The reference program's roundings to bfloat16 on the way count: a program that leaves them out, or rounds other values in their place, can miss the bound.
Values may be sent and summed in bfloat16 or wider, within the bound.
A program may use at most 192 MiB of HBM per device.

```python
import math
import jax
import jax.numpy as jnp
import numpy as np
from jax import lax

D = 384
HEADS = 6
H = 1536
SEQ = 197
STEP = 5
TOK_DEV = 788
IMAGES = 128
TOKENS = 25216
EXPERTS = 8
CAP = 295
N_HEAD = 4
DEVICES = 32


def draw_capacity(key, part):
    key = jax.random.fold_in(key, 37)
    keys = jax.random.split(key, 2)
    values = jax.random.randint(keys[0], (EXPERTS,), (CAP + 1) // 2, CAP + 1, dtype=jnp.int32)
    full = jax.random.randint(keys[1], (), 0, EXPERTS, dtype=jnp.int32)
    return values.at[full].set(CAP).astype(jnp.int32)


def draw_norm_params(key, part):
    key = jax.random.fold_in(key, 11)
    keys = jax.random.split(key, 2)
    ramp = jnp.arange(D, dtype=jnp.float32) / D
    rise = 0.5 + ramp
    noise = 1.0 + 0.1 * jnp.clip(jax.random.normal(keys[0], (D, 2)), -3.0, 3.0)
    shift = 0.3 * jnp.clip(jax.random.normal(keys[1], (D, 2)), -3.0, 3.0)
    gains = rise[:, None] * noise
    return jnp.stack([gains[:, 0], shift[:, 0], gains[:, 1], shift[:, 1]], axis=1).astype(jnp.float32)


def draw_expert_down(key, part):
    key = jax.random.fold_in(key, 23)
    ramp = jnp.arange(H, dtype=jnp.float32) / H
    scale = (0.5 + ramp) * H ** (-0.5)
    base = jnp.clip(jax.random.normal(key, (EXPERTS, D, H)), -4.0, 4.0)
    return (base * scale).astype(jnp.float32)


def shard_levels(key, shape, cuts, least, largest):
    def one(axis_at, blocks):
        heights = jax.random.uniform(jax.random.fold_in(jax.random.fold_in(key, 6), axis_at), (blocks,), jnp.float32, least / len(cuts), largest / len(cuts))
        return jnp.repeat(jnp.exp(heights), shape[axis_at] // blocks).reshape((-1,) + (1,) * (len(shape) - axis_at - 1))

    loudness = one(*cuts[0])
    for cut in cuts[1:]:
        loudness = loudness * one(*cut)
    return loudness


def shared_out(own_key, own, number, rows, number_of, top, bound, lean):
    order = jax.random.permutation(own_key, number_of)
    crowded, common = shares(number_of, rows * top, bound, lean, True), shares(number_of, rows * top, bound, lean, False)
    places = jnp.arange(number_of)

    def named(lengths, turn):
        used = int((lengths > 0).sum())
        fixed = max(1, used // 4)
        moved = fixed + (places - fixed + turn * (used - fixed)) % max(1, number_of - fixed)
        return jnp.zeros((number_of,), jnp.int32).at[order[jnp.where(places < fixed, places, moved)]].set(jnp.asarray(lengths, jnp.int32))

    lengths = jnp.where(number % 4 == 0, named(crowded, number // 4), named(common, number - number // 4 - 1))
    mixed = jax.random.permutation(jax.random.fold_in(own, 3), number_of)
    source_of, receiver = mixed[0:number_of // 2 * 2:2], mixed[1:number_of // 2 * 2:2]
    slack = jnp.minimum(lengths[source_of] - 1, bound - lengths[receiver]) // 2
    slack = jnp.where((source_of == order[0]) | (receiver == order[0]) | (lengths[receiver] == 0), 0, jnp.maximum(slack, 0))
    moved = jax.random.randint(jax.random.fold_in(own, 4), (number_of // 2,), 0, 1 << 20) % (slack + 1)
    lengths = lengths.at[source_of].add(-moved).at[receiver].add(moved)
    items = jnp.searchsorted(jnp.cumsum(lengths), jnp.arange(rows * top), side="right").astype(jnp.int32)
    table = items.reshape(top, rows).T
    table = table[jax.random.permutation(jax.random.fold_in(own, 1), rows)]
    turn = jax.random.randint(jax.random.fold_in(own, 2), (rows, 1), 0, top)
    return jnp.take_along_axis(table, (jnp.arange(top)[None, :] + turn) % top, axis=1)


def shares(count, total, limit, slope, full):
    weights = [(1 << 20) // math.isqrt(grade ** slope) + 1 for grade in range(1, count + 1)]
    largest = limit if full else min(limit, max(-(-total // count), total * weights[0] // sum(weights)))
    least = 1 if total - largest >= count - 1 else 0
    holding, surplus = [largest] + [least] * (count - 1), total - largest - least * (count - 1)
    while surplus > 0:
        movable = [i for i in range(1, count) if holding[i] < largest] or [i for i in range(1, count) if holding[i] < limit]
        pool, remaining = sum([weights[i] for i in movable]), surplus
        for i in movable:
            extra = min(limit - holding[i], max(1, remaining * weights[i] // pool), surplus)
            holding[i] = holding[i] + extra
            surplus = surplus - extra
    return np.array(holding)


def centred(own_key, dims, width, reach, shards=(), held_as=jnp.bfloat16):
    array = jax.random.normal(own_key, dims, jnp.float32) * width
    if len(shards) > 0:
        array = shard_levels(own_key, dims, shards, -0.22, 0.18) * array
    return jnp.clip(array, min=-reach, max=reach).astype(held_as)


def setup_inputs(seed: int = 0) -> dict:
    key_list = jax.random.split(jax.random.key(seed), 23)
    block_input = centred(key_list[0], (TOKENS, D), 1.0, 6.0, ((0, 32),))
    out_cotangent = centred(key_list[1], (TOKENS, D), 1.0, 6.0, ((0, 32),))
    route_ids_keys = jax.random.split(jax.random.fold_in(key_list[2], 1), TOKENS // TOK_DEV)
    route_ids_turns = jax.random.permutation(jax.random.fold_in(key_list[2], 3), TOKENS // TOK_DEV)
    route_ids = jax.vmap(lambda own, number: shared_out(jax.random.fold_in(key_list[2], 2), own, number, TOK_DEV, EXPERTS, 2, 2 * CAP, 2))(route_ids_keys, route_ids_turns).reshape((TOKENS, 2))
    capacity = draw_capacity(jax.random.fold_in(key_list[22], 71), 0)
    qkv_weight = centred(key_list[4], (D, 3 * D), (1.3 * D ** -0.5), 0.375, ((0, 4),), jnp.float32)
    qkv_first = centred(key_list[5], (D, 3 * D), (0.055 * (DEVICES * TOK_DEV) ** 0.5), 56.0, ((0, 4),), jnp.float32)
    qkv_second = jnp.clip(jnp.exp(math.log(25.216) - 1.3862944 * jax.random.uniform(key_list[6], (D, 3 * D), jnp.float32) ** shard_levels(key_list[6], (D, 3 * D), ((0, 4),), -0.2, 0.2)), 6.304, 25.216)
    proj_weight = centred(key_list[7], (D, D), (4.0 * D ** -0.5), 1.25, ((0, 4),), jnp.float32)
    proj_first = centred(key_list[8], (D, D), (0.028 * (DEVICES * TOK_DEV) ** 0.5), 28.0, ((0, 4),), jnp.float32)
    proj_second = jnp.clip(jnp.exp(math.log(6.304) - 1.3862944 * jax.random.uniform(key_list[9], (D, D), jnp.float32) ** shard_levels(key_list[9], (D, D), ((0, 4),), -0.2, 0.2)), 1.576, 6.304)
    router_weight = centred(key_list[10], (D, EXPERTS), (0.8 * D ** -0.5), 0.25, ((0, 4),), jnp.float32)
    router_first = centred(key_list[11], (D, EXPERTS), (0.44 * (2 * N_HEAD * TOK_DEV) ** 0.5), 224.0, ((0, 4),), jnp.float32)
    router_second = jnp.clip(jnp.exp(math.log(403.456) - 1.3862944 * jax.random.uniform(key_list[12], (D, EXPERTS), jnp.float32) ** shard_levels(key_list[12], (D, EXPERTS), ((0, 4),), -0.2, 0.2)), 100.864, 403.456)
    norm_params = draw_norm_params(jax.random.fold_in(key_list[22], 71), 0)
    norm_first = centred(key_list[14], (D, 4), (0.055 * (DEVICES * TOK_DEV) ** 0.5), 56.0, ((0, 4),), jnp.float32)
    norm_second = jnp.clip(jnp.exp(math.log(25.216) - 1.3862944 * jax.random.uniform(key_list[15], (D, 4), jnp.float32) ** shard_levels(key_list[15], (D, 4), ((0, 4),), -0.2, 0.2)), 6.304, 25.216)
    expert_up = centred(key_list[16], (EXPERTS, D, H), D ** -0.5, 0.3125, ((0, 8), (2, 4)), jnp.float32)
    up_first = centred(key_list[17], (EXPERTS, D, H), (0.017 * (2 * N_HEAD * TOK_DEV) ** 0.5), 8.0, ((0, 8), (2, 4)), jnp.float32)
    up_second = jnp.clip(jnp.exp(math.log(0.56736) - 1.3862944 * jax.random.uniform(key_list[18], (EXPERTS, D, H), jnp.float32) ** shard_levels(key_list[18], (EXPERTS, D, H), ((0, 8), (2, 4)), -0.2, 0.2)), 0.14184, 0.56736)
    expert_down = draw_expert_down(jax.random.fold_in(key_list[22], 71), 0)
    down_first = centred(key_list[20], (EXPERTS, D, H), (0.033 * (2 * N_HEAD * TOK_DEV) ** 0.5), 16.0, ((0, 8), (2, 4)), jnp.float32)
    down_second = jnp.clip(jnp.exp(math.log(2.26944) - 1.3862944 * jax.random.uniform(key_list[21], (EXPERTS, D, H), jnp.float32) ** shard_levels(key_list[21], (EXPERTS, D, H), ((0, 8), (2, 4)), -0.2, 0.2)), 0.56736, 2.26944)
    return {"block_input": block_input, "out_cotangent": out_cotangent, "route_ids": route_ids, "capacity": capacity, "qkv_weight": qkv_weight, "qkv_first": qkv_first, "qkv_second": qkv_second, "proj_weight": proj_weight, "proj_first": proj_first, "proj_second": proj_second, "router_weight": router_weight, "router_first": router_first, "router_second": router_second, "norm_params": norm_params, "norm_first": norm_first, "norm_second": norm_second, "expert_up": expert_up, "up_first": up_first, "up_second": up_second, "expert_down": expert_down, "down_first": down_first, "down_second": down_second}


@jax.custom_vjp
def low(v):
    return lax.optimization_barrier(v.astype(jnp.bfloat16)).astype(jnp.float32)

@jax.custom_vjp
def low_back(v):
    return v

def low_keep(v):
    return (low(v), None)

def low_pass(kept, grad):
    return (grad,)

def back_keep(v):
    return (v, None)

def back_low(kept, grad):
    return (low(grad),)
low.defvjp(low_keep, low_pass)
low_back.defvjp(back_keep, back_low)
beta_one = 0.9
beta_two = 0.999
adam_eps = 1e-06
decay_rate = 0.01
learn_rate = 0.4
norm_eps = 1e-06

def layer_norm(values, gain, shift):
    center = values - lax.optimization_barrier(jnp.mean(values, axis=-1, keepdims=True))
    scale = lax.rsqrt(lax.optimization_barrier(jnp.mean(center * center, axis=-1, keepdims=True)) + norm_eps)
    return center * scale * gain + shift

def gelu_exact(values):
    return jax.nn.gelu(values, approximate=False)

def adam_terms(weight, grad, first, second):
    new_first = beta_one * first + (1.0 - beta_one) * grad
    new_second = beta_two * second + (1.0 - beta_two) * grad * grad
    corr_one = 1.0 - beta_one ** STEP
    corr_two = 1.0 - beta_two ** STEP
    update = new_first / corr_one / (jnp.sqrt(new_second / corr_two) + adam_eps) + decay_rate * weight
    return (new_first, new_second, update)

def squares(values):
    return jnp.sum(values * values)

def attention_rows(rows, qkv_w, proj_w, norm_p):
    count = rows.shape[0]
    images = count // SEQ
    head_size = D // HEADS
    first = low(layer_norm(rows, norm_p[:, 0], norm_p[:, 1]))
    triple = low(low_back(jnp.dot(first, qkv_w, precision=lax.Precision.HIGHEST)))
    triple = triple.reshape(images, SEQ, 3, HEADS, head_size)
    query, key, value = (triple[:, :, 0], triple[:, :, 1], triple[:, :, 2])
    scores = low_back(jnp.einsum('isnd,itnd->inst', query, key, precision=lax.Precision.HIGHEST) * head_size ** (-0.5))
    weights = low(jax.nn.softmax(scores, axis=-1))
    mixed = low(low_back(jnp.einsum('inst,itnd->isnd', weights, value, precision=lax.Precision.HIGHEST)))
    mixed = mixed.reshape(count, D)
    return rows + low_back(jnp.dot(mixed, proj_w, precision=lax.Precision.HIGHEST))

def reference(block_input, out_cotangent, route_ids, capacity, qkv_weight, qkv_first, qkv_second, proj_weight, proj_first, proj_second, router_weight, router_first, router_second, norm_params, norm_first, norm_second, expert_up, up_first, up_second, expert_down, down_first, down_second):
    device_of = jnp.arange(TOKENS, dtype=jnp.int32) // TOK_DEV
    ordered = route_ids.reshape(DEVICES, TOK_DEV, 2).transpose(0, 2, 1).reshape(DEVICES, 2 * TOK_DEV)
    onehot = (ordered[:, :, None] == jnp.arange(EXPERTS, dtype=jnp.int32)[None, None, :]).astype(jnp.int32)
    slot = lax.optimization_barrier(jnp.sum((jnp.cumsum(onehot, axis=1) - onehot) * onehot, axis=2))
    slot = slot.reshape(DEVICES, 2, TOK_DEV).transpose(0, 2, 1).reshape(TOKENS, 2)
    kept = slot < capacity[route_ids]
    keptf = kept.astype(jnp.float32)
    dest = jnp.where(kept, route_ids * (DEVICES * CAP) + device_of[:, None] * CAP + slot, EXPERTS * DEVICES * CAP)
    table = jnp.full((EXPERTS * DEVICES * CAP,), 2 * TOKENS, jnp.int32)
    table = table.at[dest.reshape(-1)].set(jnp.arange(2 * TOKENS, dtype=jnp.int32), mode='drop')
    table = table.reshape(EXPERTS, DEVICES * CAP)
    group = 16 if IMAGES % 16 == 0 else 1

    def forward(rows, qkv_w, proj_w, router_w, norm_p, up_w, down_w):
        qkv_w, proj_w, router_w, norm_p, up_w, down_w = [low(w) for w in (qkv_w, proj_w, router_w, norm_p, up_w, down_w)]

        def image_step(carry, block):
            return (carry, attention_rows(block, qkv_w, proj_w, norm_p))
        blocks = rows.reshape(IMAGES // group, group * SEQ, D)
        _, resid = lax.scan(jax.checkpoint(image_step), jnp.zeros((), jnp.float32), blocks)
        resid = resid.reshape(TOKENS, D)
        second = low(layer_norm(resid, norm_p[:, 2], norm_p[:, 3]))
        logits = low_back(jnp.dot(second, router_w, precision=lax.Precision.HIGHEST))
        chosen = jnp.take_along_axis(logits, route_ids, axis=1)
        weighted = (jax.nn.softmax(chosen, axis=-1) * keptf).reshape(-1)

        def compute(index, up_e, down_e):
            token = jnp.minimum(index // 2, TOKENS - 1)
            picked = low_back(second[token])
            pre = low_back(jnp.dot(picked, up_e, precision=lax.Precision.HIGHEST))
            hidden = low(gelu_exact(pre))
            result = low(low_back(jnp.dot(hidden, down_e.T, precision=lax.Precision.HIGHEST)))
            share = weighted[jnp.minimum(index, 2 * TOKENS - 1)] * (index < 2 * TOKENS).astype(jnp.float32)
            return result * share[:, None]

        def expert_step(carry, pieces):
            index, up_e, down_e = pieces
            contrib = jax.checkpoint(compute)(index, up_e, down_e)
            return (carry.at[index // 2].add(contrib, mode='drop'), None)
        delta, _ = lax.scan(expert_step, jnp.zeros((TOKENS, D), jnp.float32), (table, up_w, down_w))
        return resid + delta
    output, pullback = jax.vjp(forward, block_input.astype(jnp.float32), qkv_weight, proj_weight, router_weight, norm_params, expert_up, expert_down)
    grad_in, grad_qkv, grad_proj, grad_router, grad_norm, grad_up, grad_down = pullback(out_cotangent.astype(jnp.float32))
    qkv_m, qkv_v, qkv_r = adam_terms(qkv_weight, grad_qkv, qkv_first, qkv_second)
    proj_m, proj_v, proj_r = adam_terms(proj_weight, grad_proj, proj_first, proj_second)
    router_m, router_v, router_r = adam_terms(router_weight, grad_router, router_first, router_second)
    norm_m, norm_v, norm_r = adam_terms(norm_params, grad_norm, norm_first, norm_second)
    up_m, up_v, up_r = adam_terms(expert_up, grad_up, up_first, up_second)
    down_m, down_v, down_r = adam_terms(expert_down, grad_down, down_first, down_second)
    weight_col = jnp.concatenate([jnp.stack([squares(qkv_weight), squares(proj_weight), squares(router_weight)]), lax.optimization_barrier(jnp.sum(norm_params * norm_params, axis=0))])
    update_col = jnp.concatenate([jnp.stack([squares(qkv_r), squares(proj_r), squares(router_r)]), lax.optimization_barrier(jnp.sum(norm_r * norm_r, axis=0))])
    dense_norms = jnp.sqrt(jnp.stack([weight_col, update_col], axis=1))
    expert_norms = jnp.sqrt(jnp.stack([lax.optimization_barrier(jnp.sum(expert_up * expert_up, axis=(1, 2))), lax.optimization_barrier(jnp.sum(up_r * up_r, axis=(1, 2))), lax.optimization_barrier(jnp.sum(expert_down * expert_down, axis=(1, 2))), lax.optimization_barrier(jnp.sum(down_r * down_r, axis=(1, 2)))], axis=1))
    trust = dense_norms[:, 0] / dense_norms[:, 1]
    qkv_new = qkv_weight - learn_rate * trust[0] * qkv_r
    proj_new = proj_weight - learn_rate * trust[1] * proj_r
    router_new = router_weight - learn_rate * trust[2] * router_r
    norm_new = norm_params - learn_rate * trust[3:][None, :] * norm_r
    up_new = expert_up - learn_rate * (expert_norms[:, 0] / expert_norms[:, 1])[:, None, None] * up_r
    down_new = expert_down - learn_rate * (expert_norms[:, 2] / expert_norms[:, 3])[:, None, None] * down_r
    return (output.astype(jnp.bfloat16), grad_in.astype(jnp.bfloat16), qkv_new, qkv_new.astype(jnp.bfloat16), qkv_m, qkv_v, proj_new, proj_new.astype(jnp.bfloat16), proj_m, proj_v, router_new, router_new.astype(jnp.bfloat16), router_m, router_v, norm_new, norm_new.astype(jnp.bfloat16), norm_m, norm_v, up_new, up_new.astype(jnp.bfloat16), up_m, up_v, down_new, down_new.astype(jnp.bfloat16), down_m, down_v, dense_norms, expert_norms)
```

```python
import functools
import jax
import jax.numpy as jnp
from jax import lax
from jax.experimental import pallas as pl
from jax.experimental.pallas import tpu as pltpu
from jax.sharding import PartitionSpec as P

HEADS = 6
SEQ = 197
STEP = 5
ROWS = 208
KEYS = 256
LANES = 128

beta_one = 0.9
beta_two = 0.999
adam_eps = 1e-06
decay_rate = 0.01
learn_rate = 0.4
norm_eps = 1e-06

F32 = jnp.float32
BF16 = jnp.bfloat16
VMEM = pl.BlockSpec(memory_space=pltpu.VMEM)


def nn(left, right):
    return lax.dot_general(left, right, (((1,), (0,)), ((), ())), preferred_element_type=F32)


def nt(left, right):
    return lax.dot_general(left, right, (((1,), (1,)), ((), ())), preferred_element_type=F32)


def tn(left, right):
    return lax.dot_general(left, right, (((0,), (0,)), ((), ())), preferred_element_type=F32)


def params(mib=56, **more):
    return pltpu.CompilerParams(vmem_limit_bytes=mib * 2**20, **more)


def ceil_to(value, step):
    return -(-value // step) * step


def normed(values):
    center = values - jnp.mean(values, axis=1, keepdims=True)
    scale = lax.rsqrt(jnp.mean(center * center, axis=1, keepdims=True) + norm_eps)
    return center * scale, scale


def lane_index(rows, lanes):
    return lax.broadcasted_iota(jnp.int32, (rows, lanes), 1)


def attend_body(images, experts, slots, refs):
    (
        tokens, dout, routes, limits, norms, qkv, proj, router,
        first, triple, logsum, mixed, resid, second, pos, gates, sent,
        whole, dpad, wide, picked, weighted,
    ) = refs
    count = images * SEQ
    total = images * ROWS
    width = tokens.shape[1]
    head_size = width // HEADS
    scale = head_size ** (-0.5)
    wide[0:count, :] = tokens[...].astype(F32)
    whole[...] = jnp.zeros_like(whole)
    for i in range(images):
        whole[i * ROWS : i * ROWS + SEQ, :] = wide[i * SEQ : (i + 1) * SEQ, :]
    wide[0:count, :] = dout[...].astype(F32)
    for i in range(images):
        dpad[i * ROWS : (i + 1) * ROWS, :] = jnp.concatenate(
            [wide[i * SEQ : (i + 1) * SEQ, :], jnp.zeros((ROWS - SEQ, width), F32)], axis=0
        ).astype(BF16)
    ids = routes[...].astype(F32)
    picked[...] = jnp.full(picked.shape, -1.0, F32)
    for i in range(images):
        picked[i * ROWS : i * ROWS + SEQ, 0:2] = ids[i * SEQ : (i + 1) * SEQ, :]
    lanes = lane_index(total, LANES).astype(F32)
    one = jnp.where(lanes == picked[:, 0:1], 1.0, 0.0)
    two = jnp.where(lanes == picked[:, 1:2], 1.0, 0.0)
    firsts = jnp.sum(one, axis=0, keepdims=True)
    both = jnp.concatenate([one.astype(BF16), two.astype(BF16)], axis=1)
    gain_one, shift_one = norms[0:1, :], norms[1:2, :]
    gain_two, shift_two = norms[2:3, :], norms[3:4, :]
    triple[total:, :] = jnp.zeros((triple.shape[0] - total, triple.shape[1]), BF16)

    def project(i, carry):
        rows = pl.ds(pl.multiple_of(i * ROWS, 16), ROWS)
        ready = (normed(whole[rows, :])[0] * gain_one + shift_one).astype(BF16)
        first[rows, :] = ready
        triple[rows, :] = nn(ready, qkv[...]).astype(BF16)
        return carry

    lax.fori_loop(0, images, project, 0)
    low = lane_index(1, LANES) < head_size
    real = lane_index(1, KEYS) < SEQ
    spot = lane_index(1, LANES)

    def image(i, carry):
        start = pl.multiple_of(i * ROWS, 16)
        rows = pl.ds(start, ROWS)
        keys = pl.ds(start, KEYS)
        sums = jnp.zeros((ROWS, LANES), F32)
        for pair in range(HEADS // 2):
            at = pair * 2 * head_size
            query = triple[rows, at : at + LANES]
            key = triple[keys, width + at : width + at + LANES]
            value = triple[keys, 2 * width + at : 2 * width + at + LANES]
            blend = jnp.zeros((ROWS, LANES), F32)
            for side in range(2):
                mine = low if side == 0 else jnp.logical_not(low)
                scores = nt(query, jnp.where(mine, key, 0.0).astype(BF16)) * scale
                scores = jnp.where(real, scores, -1e30)
                top = jnp.max(scores, axis=1, keepdims=True)
                expo = jnp.exp(scores - top)
                summed = jnp.sum(expo, axis=1, keepdims=True)
                sums = jnp.where(spot == pair * 2 + side, top + jnp.log(summed), sums)
                weights = (expo * (1.0 / summed)).astype(BF16)
                blend = blend + nn(weights, jnp.where(mine, value, 0.0).astype(BF16))
            mixed[rows, at : at + LANES] = blend.astype(BF16)
        logsum[rows, :] = sums
        after = whole[rows, :] + nn(mixed[rows, :], proj[...])
        resid[rows, :] = after
        ready = (normed(after)[0] * gain_two + shift_two).astype(BF16)
        second[rows, :] = ready
        logits = nn(ready, router[...])
        lane = lane_index(ROWS, LANES).astype(F32)
        choose = picked[rows, :]
        hot_one = lane == choose[:, 0:1]
        hot_two = lane == choose[:, 1:2]
        level_one = jnp.sum(jnp.where(hot_one, logits, 0.0), axis=1, keepdims=True)
        level_two = jnp.sum(jnp.where(hot_two, logits, 0.0), axis=1, keepdims=True)
        top = jnp.maximum(level_one, level_two)
        expo_one = jnp.exp(level_one - top)
        expo_two = jnp.exp(level_two - top)
        summed = expo_one + expo_two
        gate = jnp.where(hot_one, expo_one / summed, jnp.where(hot_two, expo_two / summed, 0.0))
        gates[rows, :] = gate
        column = lax.broadcasted_iota(jnp.int32, (ROWS, total), 1)
        row = lax.broadcasted_iota(jnp.int32, (ROWS, total), 0) + start
        earlier = nn(jnp.where(column < row, 1.0, 0.0).astype(BF16), both)
        slot = jnp.where(hot_one, earlier[:, :LANES], earlier[:, LANES:] + firsts)
        kept = jnp.logical_and(jnp.logical_or(hot_one, hot_two), slot < limits[...])
        pos[rows, :] = jnp.where(kept, slot, -1.0)
        weighted[rows, :] = jnp.where(kept, gate, 0.0)
        return carry

    lax.fori_loop(0, images, image, 0)
    across = jnp.transpose(pos[...])
    weights_across = jnp.transpose(weighted[...])
    picked_rows = across.shape[0]
    pos_rows, weight_rows = across, weights_across
    for e in range(experts):
        slot = lax.broadcasted_iota(jnp.int32, (slots, total), 0).astype(F32)
        hit = slot == pos_rows[e : e + 1, :]
        share = jnp.sum(jnp.where(hit, weight_rows[e : e + 1, :], 0.0), axis=1, keepdims=True)
        place = jnp.where(hit, 1.0, 0.0).astype(BF16)
        sent[e, :, 0:width] = nn(place, second[...]).astype(BF16)
        sent[e, :, width:] = (nn(place, dpad[...]) * share).astype(BF16)


def attend(tokens, dout, routes, limits, norms, qkv, proj, router, experts, slots):
    count, width = tokens.shape
    images = count // SEQ
    total = images * ROWS
    shape = jax.ShapeDtypeStruct
    return pl.pallas_call(
        lambda *refs: attend_body(images, experts, slots, refs),
        out_shape=(
            shape((total, width), BF16),
            shape((total + KEYS - ROWS, 3 * width), BF16),
            shape((total, LANES), F32),
            shape((total, width), BF16),
            shape((total, width), F32),
            shape((total, width), BF16),
            shape((total, LANES), F32),
            shape((total, LANES), F32),
            shape((experts, slots, 2 * width), BF16),
        ),
        in_specs=[VMEM] * 8,
        out_specs=tuple([VMEM] * 9),
        scratch_shapes=[
            pltpu.VMEM((total, width), F32),
            pltpu.VMEM((total, width), BF16),
            pltpu.VMEM((ceil_to(count, 8), width), F32),
            pltpu.VMEM((total, LANES), F32),
            pltpu.VMEM((total, LANES), F32),
        ],
        compiler_params=params(),
        name="attend",
    )(tokens, dout, routes, limits, norms, qkv, proj, router)


def gelu_pair(pre):
    half = 0.5 + 0.5 * lax.erf(pre * 0.7071067811865476)
    slope = half + pre * (jnp.exp(pre * pre * -0.5) * 0.3989422804014327)
    return pre * half, slope


def chunk_rows(total):
    size = 320
    while total % size:
        size -= 16
    return size


def expert_body(rows, chunk, tile, refs):
    (arrived, up, down, back, grad_up, grad_down, hidden_all, dpre_all) = refs
    width = up.shape[0]
    hidden_size = up.shape[1]

    def block(b, carry):
        at = pl.ds(pl.multiple_of(b * chunk, 16), chunk)
        x = arrived[at, 0:width]
        da = arrived[at, width:]
        answer = jnp.zeros((chunk, width), F32)
        drow = jnp.zeros((chunk, width), F32)
        for j in range(hidden_size // tile):
            cols = slice(j * tile, (j + 1) * tile)
            hidden, slope = gelu_pair(nn(x, up[:, cols]))
            hidden = hidden.astype(BF16)
            dpre = (nn(da, down[:, cols]) * slope).astype(BF16)
            hidden_all[at, cols] = hidden
            dpre_all[at, cols] = dpre
            answer = answer + nt(hidden, down[:, cols])
            drow = drow + nt(dpre, up[:, cols])
        back[at, 0:width] = answer.astype(BF16)
        back[at, width:] = drow.astype(BF16)
        return carry

    lax.fori_loop(0, rows // chunk, block, 0)

    def grads(j, carry):
        cols = pl.ds(pl.multiple_of(j * 256, 256), 256)
        grad_up[:, cols] = tn(arrived[:, 0:width], dpre_all[:, cols])
        grad_down[:, cols] = tn(arrived[:, width:], hidden_all[:, cols])
        return carry

    lax.fori_loop(0, hidden_size // 256, grads, 0)


def expert(arrived, up, down):
    rows = arrived.shape[0]
    width, hidden = up.shape
    chunk = chunk_rows(rows)
    shape = jax.ShapeDtypeStruct
    return pl.pallas_call(
        lambda *refs: expert_body(rows, chunk, 512, refs),
        out_shape=(
            shape((rows, 2 * width), BF16),
            shape((width, hidden), F32),
            shape((width, hidden), F32),
        ),
        in_specs=[VMEM] * 3,
        out_specs=(VMEM, VMEM, VMEM),
        scratch_shapes=[pltpu.VMEM((rows, hidden), BF16), pltpu.VMEM((rows, hidden), BF16)],
        compiler_params=params(),
        name="expert",
    )(arrived, up, down)


def norm_back(grad, values, gain):
    xhat, scale = normed(values)
    dgain = jnp.sum(grad * xhat, axis=0, keepdims=True)
    dshift = jnp.sum(grad, axis=0, keepdims=True)
    inner = grad * gain
    mean_one = jnp.mean(inner, axis=1, keepdims=True)
    mean_two = jnp.mean(inner * xhat, axis=1, keepdims=True)
    return (inner - mean_one - xhat * mean_two) * scale, dgain, dshift


def back_body(images, experts, slots, refs):
    (
        tokens, dout, norms, qkv, proj, router,
        first, triple, logsum, mixed, resid, second, pos, gates, back,
        output, input_grad, grads,
        wide, whole, dpad, outs, dwe, drow, dtriple, dres, dkeys, dvals, dmix, small,
    ) = refs
    count = images * SEQ
    total = images * ROWS
    width = tokens.shape[1]
    head_size = width // HEADS
    scale = head_size ** (-0.5)
    gain_one, gain_two = norms[0:1, :], norms[2:3, :]
    wide[0:count, :] = tokens[...].astype(F32)
    whole[...] = jnp.zeros_like(whole)
    for i in range(images):
        whole[i * ROWS : i * ROWS + SEQ, :] = wide[i * SEQ : (i + 1) * SEQ, :]
    wide[0:count, :] = dout[...].astype(F32)
    dpad[...] = jnp.zeros_like(dpad)
    for i in range(images):
        dpad[i * ROWS : i * ROWS + SEQ, :] = wide[i * SEQ : (i + 1) * SEQ, :]
    outs[...] = resid[...]
    dwe[...] = jnp.zeros_like(dwe)
    drow[...] = jnp.zeros_like(drow)
    lane = lane_index(ROWS, LANES)
    slot = lane_index(ROWS, slots).astype(F32)

    def combine(i, carry):
        rows = pl.ds(pl.multiple_of(i * ROWS, 16), ROWS)
        dhere = dpad[rows, :]
        out = resid[rows, :]
        dws = jnp.zeros((ROWS, LANES), F32)
        dr = jnp.zeros((ROWS, width), F32)
        place_at = pos[rows, :]
        gate = gates[rows, :]
        for e in range(experts):
            at = place_at[:, e : e + 1]
            place = jnp.where(slot == at, 1.0, 0.0).astype(BF16)
            both = nn(place, back[e])
            answer = both[:, 0:width]
            share = jnp.where(at >= 0.0, gate[:, e : e + 1], 0.0)
            out = out + share * answer
            dws = jnp.where(lane == e, jnp.sum(dhere * answer, axis=1, keepdims=True), dws)
            dr = dr + both[:, width:]
        outs[rows, :] = out
        dchosen = gate * (dws - jnp.sum(gate * dws, axis=1, keepdims=True))
        dlogits = dchosen.astype(BF16)
        dwe[rows, :] = dlogits
        drow[rows, :] = dr + nt(dlogits, router[...])
        return carry

    lax.fori_loop(0, images, combine, 0)
    for i in range(images):
        wide[i * SEQ : (i + 1) * SEQ, :] = outs[i * ROWS : i * ROWS + SEQ, :]
    output[...] = wide[0:count, :].astype(BF16)
    small[...] = jnp.zeros_like(small)

    def second_norm(i, carry):
        rows = pl.ds(pl.multiple_of(i * ROWS, 16), ROWS)
        dx, dgain, dshift = norm_back(drow[rows, :], resid[rows, :], gain_two)
        dx = dx + dpad[rows, :]
        small[2:3, :] += dgain
        small[3:4, :] += dshift
        dres[rows, :] = dx
        dattn = dx.astype(BF16)
        drow[rows, :] = dx
        dmix[rows, :] = nt(dattn, proj[...]).astype(BF16)
        return carry

    lax.fori_loop(0, images, second_norm, 0)
    low = lane_index(1, LANES) < head_size
    real = lane_index(1, KEYS) < SEQ
    zero = jnp.zeros((), BF16)

    def image(i, carry):
        start = pl.multiple_of(i * ROWS, 16)
        rows = pl.ds(start, ROWS)
        keys = pl.ds(start, KEYS)
        sums = logsum[rows, :]
        for pair in range(HEADS // 2):
            at = pair * 2 * head_size
            query = triple[rows, at : at + LANES]
            key = triple[keys, width + at : width + at + LANES]
            value = triple[keys, 2 * width + at : 2 * width + at + LANES]
            dm = dmix[rows, at : at + LANES]
            dq = jnp.zeros((ROWS, LANES), F32)
            dk = jnp.zeros((KEYS, LANES), F32)
            dv = jnp.zeros((KEYS, LANES), F32)
            for side in range(2):
                mine = low if side == 0 else jnp.logical_not(low)
                head = pair * 2 + side
                key_mine = jnp.where(mine, key, zero)
                scores = nt(query, key_mine) * scale
                probs = jnp.where(real, jnp.exp(scores - sums[:, head : head + 1]), 0.0)
                dprobs = nt(jnp.where(mine, dm, zero), value)
                inner = jnp.sum(dprobs * probs, axis=1, keepdims=True)
                dscores = (probs * (dprobs - inner)).astype(BF16)
                dv = dv + tn(probs.astype(BF16), jnp.where(mine, dm, zero))
                dq = dq + nn(dscores, key_mine)
                dk = dk + tn(dscores, jnp.where(mine, query, zero))
            dtriple[rows, at : at + LANES] = (dq * scale).astype(BF16)
            dtriple[rows, width + at : width + at + LANES] = (dk * scale)[:ROWS].astype(BF16)
            dtriple[rows, 2 * width + at : 2 * width + at + LANES] = dv[:ROWS].astype(BF16)
        dfirst = nt(dtriple[rows, :], qkv[...])
        dx, dgain, dshift = norm_back(dfirst, whole[rows, :], gain_one)
        small[0:1, :] += dgain
        small[1:2, :] += dshift
        dres[rows, :] += dx
        return carry

    lax.fori_loop(0, images, image, 0)
    for i in range(images):
        wide[i * SEQ : (i + 1) * SEQ, :] = dres[i * ROWS : i * ROWS + SEQ, :]
    input_grad[...] = wide[0:count, :].astype(BF16)
    grads[:, 0 : 3 * width] = tn(first[...], dtriple[...])
    grads[:, 3 * width : 4 * width] = tn(mixed[...], drow[...].astype(BF16))
    tail = tn(second[...], dwe[...])
    columns = jnp.transpose(jnp.concatenate([small[...], jnp.zeros((LANES - 8, width), F32)], axis=0))
    shifted = pltpu.roll(columns, experts, 1)
    grads[:, 4 * width :] = jnp.where(lane_index(width, LANES) < experts, tail, shifted)


def backward(tokens, dout, norms, qkv, proj, router, saved, back, experts, slots):
    count, width = tokens.shape
    images = count // SEQ
    total = images * ROWS
    shape = jax.ShapeDtypeStruct
    return pl.pallas_call(
        lambda *refs: back_body(images, experts, slots, refs),
        out_shape=(
            shape((count, width), BF16),
            shape((count, width), BF16),
            shape((width, 4 * width + LANES), F32),
        ),
        in_specs=[VMEM] * 15,
        out_specs=(VMEM, VMEM, VMEM),
        scratch_shapes=[
            pltpu.VMEM((ceil_to(count, 8), width), F32),
            pltpu.VMEM((total, width), F32),
            pltpu.VMEM((total, width), F32),
            pltpu.VMEM((total, width), F32),
            pltpu.VMEM((total, LANES), BF16),
            pltpu.VMEM((total, width), F32),
            pltpu.VMEM((total, 3 * width), BF16),
            pltpu.VMEM((total, width), F32),
            pltpu.VMEM((8, LANES), BF16),
            pltpu.VMEM((8, LANES), BF16),
            pltpu.VMEM((total, width), BF16),
            pltpu.VMEM((8, width), F32),
        ],
        compiler_params=params(),
        name="backward",
    )(tokens, dout, norms, qkv, proj, router, *saved, back)


def squares(values):
    return jnp.sum(values * values)


def adam_terms(weight, grad, first, second):
    new_first = beta_one * first + (1.0 - beta_one) * grad
    new_second = beta_two * second + (1.0 - beta_two) * grad * grad
    corr_one = 1.0 - beta_one**STEP
    corr_two = 1.0 - beta_two**STEP
    update = (
        new_first / corr_one / (jnp.sqrt(new_second / corr_two) + adam_eps) + decay_rate * weight
    )
    return (new_first, new_second, update)


def local(
    block_input, out_cotangent, route_ids, capacity,
    qkv_weight, qkv_first, qkv_second,
    proj_weight, proj_first, proj_second,
    router_weight, router_first, router_second,
    norm_params, norm_first, norm_second,
    expert_up, up_first, up_second,
    expert_down, down_first, down_second,
):
    count, width = block_input.shape
    experts = router_weight.shape[1]
    capsize = max(2, 3 * count // lax.axis_size("expert"))
    slots = ceil_to(capsize, 16)
    rows_dev = qkv_weight.shape[0]
    dense = jnp.concatenate(
        [qkv_weight, proj_weight, router_weight, norm_params,
         jnp.zeros((rows_dev, LANES - experts - 4), F32)], axis=1
    ).astype(BF16)
    dense = lax.all_gather(dense, "head", axis=0, tiled=True)
    up_w = lax.all_gather(expert_up[0].astype(BF16), "head", axis=1, tiled=True)
    down_w = lax.all_gather(expert_down[0].astype(BF16), "head", axis=1, tiled=True)
    qkv = dense[:, 0 : 3 * width]
    proj = dense[:, 3 * width : 4 * width]
    tail = dense[:, 4 * width :]
    router = jnp.where(jnp.arange(LANES)[None, :] < experts, tail, 0)
    norms = jnp.pad(tail[:, experts : experts + 4].astype(F32).T, ((0, 4), (0, 0)))
    limits = jnp.pad(capacity.astype(F32), (0, LANES - experts))[None, :]
    *saved, sent = attend(
        block_input, out_cotangent, route_ids, limits, norms, qkv, proj, router, experts, slots
    )
    arrived = lax.all_to_all(sent, "expert", split_axis=0, concat_axis=0, tiled=True)
    back, grad_up, grad_down = expert(arrived.reshape(experts * slots, 2 * width), up_w, down_w)
    back = lax.all_to_all(
        back.reshape(experts, slots, 2 * width), "expert", split_axis=0, concat_axis=0, tiled=True
    )
    block_output, input_grad, grads = backward(
        block_input, out_cotangent, norms, qkv, proj, router, saved, back, experts, slots
    )
    summed = lax.psum_scatter(grads, "head", scatter_dimension=0, tiled=True)
    summed = lax.psum(summed, "expert")
    shares = (
        summed[:, 0 : 3 * width],
        summed[:, 3 * width : 4 * width],
        summed[:, 4 * width : 4 * width + experts],
        summed[:, 4 * width + experts : 4 * width + experts + 4],
    )
    expert_grads = (
        lax.psum_scatter(grad_up, "head", scatter_dimension=1, tiled=True),
        lax.psum_scatter(grad_down, "head", scatter_dimension=1, tiled=True),
    )
    qkv_m, qkv_v, qkv_r = adam_terms(qkv_weight, shares[0], qkv_first, qkv_second)
    proj_m, proj_v, proj_r = adam_terms(proj_weight, shares[1], proj_first, proj_second)
    router_m, router_v, router_r = adam_terms(router_weight, shares[2], router_first, router_second)
    norm_m, norm_v, norm_r = adam_terms(norm_params, shares[3], norm_first, norm_second)
    up_m, up_v, up_r = adam_terms(expert_up, expert_grads[0][None], up_first, up_second)
    down_m, down_v, down_r = adam_terms(expert_down, expert_grads[1][None], down_first, down_second)
    weight_col = jnp.concatenate(
        [
            jnp.stack([squares(qkv_weight), squares(proj_weight), squares(router_weight)]),
            jnp.sum(norm_params * norm_params, axis=0),
        ]
    )
    update_col = jnp.concatenate(
        [
            jnp.stack([squares(qkv_r), squares(proj_r), squares(router_r)]),
            jnp.sum(norm_r * norm_r, axis=0),
        ]
    )
    expert_sq = jnp.stack(
        [squares(expert_up), squares(up_r), squares(expert_down), squares(down_r)]
    )[None, :]
    totals = lax.psum((jnp.stack([weight_col, update_col], axis=1), expert_sq), "head")
    dense_norms = jnp.sqrt(totals[0])
    expert_norms = jnp.sqrt(totals[1])
    trust = dense_norms[:, 0] / dense_norms[:, 1]
    qkv_new = qkv_weight - learn_rate * trust[0] * qkv_r
    proj_new = proj_weight - learn_rate * trust[1] * proj_r
    router_new = router_weight - learn_rate * trust[2] * router_r
    norm_new = norm_params - learn_rate * trust[3:][None, :] * norm_r
    up_new = expert_up - learn_rate * (expert_norms[0, 0] / expert_norms[0, 1]) * up_r
    down_new = expert_down - learn_rate * (expert_norms[0, 2] / expert_norms[0, 3]) * down_r
    return (
        block_output, input_grad,
        qkv_new, qkv_new.astype(BF16), qkv_m, qkv_v,
        proj_new, proj_new.astype(BF16), proj_m, proj_v,
        router_new, router_new.astype(BF16), router_m, router_v,
        norm_new, norm_new.astype(BF16), norm_m, norm_v,
        up_new, up_new.astype(BF16), up_m, up_v,
        down_new, down_new.astype(BF16), down_m, down_v,
        dense_norms, expert_norms,
    )


def solution(mesh):
    tokens, dense, pair = P(("expert", "head"), None), P("head", None), P("expert", None, "head")
    return jax.shard_map(
        local,
        mesh=mesh,
        in_specs=(tokens,) * 3 + (P(),) + (dense,) * 12 + (pair,) * 6,
        out_specs=(tokens,) * 2 + (dense,) * 16 + (pair,) * 8 + (P(), P("expert", None)),
        check_vma=False,
    )
```

```python
import types

import jax
import jax.numpy as jnp
from jax import lax
from jax.experimental import pallas as pl
from jax.experimental.pallas import tpu as pltpu
from jax.sharding import PartitionSpec as P

HEADS = 6
SEQ = 197
STEP = 5
ROWS = 208
KEYS = 256
LANES = 128

beta_one = 0.9
beta_two = 0.999
adam_eps = 1e-06
decay_rate = 0.01
learn_rate = 0.4
norm_eps = 1e-06

F32 = jnp.float32
BF16 = jnp.bfloat16
VMEM = pl.BlockSpec(memory_space=pltpu.VMEM)
SMEM = pl.BlockSpec(memory_space=pltpu.SMEM)
MESH = pl.DeviceIdType.MESH


def nn(left, right):
    return lax.dot_general(left, right, (((1,), (0,)), ((), ())), preferred_element_type=F32)


def nt(left, right):
    return lax.dot_general(left, right, (((1,), (1,)), ((), ())), preferred_element_type=F32)


def tn(left, right):
    return lax.dot_general(left, right, (((0,), (0,)), ((), ())), preferred_element_type=F32)


def params(mib=58, **more):
    return pltpu.CompilerParams(vmem_limit_bytes=mib * 2**20, **more)


def ceil_to(value, step):
    return -(-value // step) * step


def normed(values):
    center = values - jnp.mean(values, axis=1, keepdims=True)
    scale = lax.rsqrt(jnp.mean(center * center, axis=1, keepdims=True) + norm_eps)
    return center * scale, scale


def lane_index(rows, lanes):
    return lax.broadcasted_iota(jnp.int32, (rows, lanes), 1)


def row_index(rows, lanes):
    return lax.broadcasted_iota(jnp.int32, (rows, lanes), 0)


def bits():
    e, h = lax.axis_index("expert"), lax.axis_index("head")
    return (e // 4, (e // 2) % 2, e % 2, h // 2, h % 2)


def device(zh, zl, y, x, c):
    return (zh * 4 + zl * 2 + y, x * 2 + c)


def flip(bit, change):
    return bit + change - 2 * bit * change


def turn(me, zh=0, zl=0, y=0, x=0, c=0):
    return tuple(flip(b, k) for b, k in zip(me, (zh, zl, y, x, c), strict=True))


def peer(me, i):
    low = (i + i // 4) % 4
    return turn(me, zl=low // 2, y=low % 2, c=i // 4)


def held_expert(where):
    return where[4] * 4 + where[1] * 2 + where[2]


def remote(src, dst, send, recv, target):
    return pltpu.make_async_remote_copy(
        src_ref=src, dst_ref=dst, send_sem=send, recv_sem=recv, device_id=target, device_id_type=MESH
    )


def greet(targets):
    barrier = pltpu.get_barrier_semaphore()
    for target in targets:
        pl.semaphore_signal(barrier, inc=1, device_id=target, device_id_type=MESH)
    pl.semaphore_wait(barrier, len(targets))


def label_matrix(experts, labels):
    row, column = row_index(LANES, LANES), lane_index(LANES, LANES)
    if labels is None:
        hit = jnp.logical_and(row == column, column < experts)
    else:
        stands = jnp.full((1, LANES), -1, jnp.int32)
        lane = lane_index(1, LANES)
        for i, e in enumerate(labels):
            stands = jnp.where(lane == i, e, stands)
        hit = row == stands
    return jnp.where(hit, 1.0, 0.0).astype(BF16)


def to_row(column, lanes):
    size = column.shape[0]
    return jnp.sum(
        jnp.where(row_index(size, lanes) == lane_index(size, lanes), column, 0.0), axis=0, keepdims=True
    )


def to_column(row, size):
    lanes = row.shape[1]
    return jnp.sum(
        jnp.where(row_index(size, lanes) == lane_index(size, lanes), row, 0.0), axis=1, keepdims=True
    )


def spread_images(images, source, wide, out):
    count = images * SEQ
    wide[0:count, :] = source[...].astype(F32)
    out[...] = jnp.zeros_like(out)
    for i in range(images):
        out[i * ROWS : i * ROWS + SEQ, :] = wide[i * SEQ : (i + 1) * SEQ, :].astype(out.dtype)


def gather_images(images, source, wide, out):
    count = images * SEQ
    for i in range(images):
        wide[i * SEQ : (i + 1) * SEQ, :] = source[i * ROWS : i * ROWS + SEQ, :]
    out[...] = wide[0:count, :].astype(out.dtype)


def route(images, experts, labels, r):
    count = images * SEQ
    total = images * ROWS
    ids = r.routes[...]
    if labels is not None:
        named_so = jnp.zeros_like(ids)
        for i, e in enumerate(labels):
            named_so = jnp.where(ids == e, i, named_so)
        ids = named_so
    r.turned[...] = jnp.zeros_like(r.turned)
    r.turned[0:2, 0:count] = ids.astype(F32)
    columns = jnp.transpose(r.turned[...])
    r.columns[...] = columns
    r.picked[...] = jnp.full(r.picked.shape, -1.0, F32)
    for i in range(images):
        r.picked[i * ROWS : i * ROWS + SEQ, :] = r.columns[i * SEQ : (i + 1) * SEQ, :]
    lane = lane_index(1, LANES)
    limits = jnp.zeros((1, LANES), F32)
    for i in range(experts):
        allowed = r.capacity[i if labels is None else labels[i]]
        limits = jnp.where(lane == i, allowed.astype(F32), limits)
    lanes = lane_index(total, LANES).astype(F32)
    one = jnp.where(lanes == r.picked[:, 0:1], 1.0, 0.0)
    two = jnp.where(lanes == r.picked[:, 1:2], 1.0, 0.0)
    firsts = jnp.sum(one, axis=0, keepdims=True)
    r.both[...] = jnp.concatenate([one.astype(BF16), two.astype(BF16)], axis=1)

    def place(i, carry):
        start = pl.multiple_of(i * ROWS, 16)
        rows = pl.ds(start, ROWS)
        lane = lane_index(ROWS, LANES).astype(F32)
        choose = r.picked[rows, :]
        hot_one = lane == choose[:, 0:1]
        hot_two = lane == choose[:, 1:2]
        before = lane_index(ROWS, total) < row_index(ROWS, total) + start
        earlier = nn(jnp.where(before, 1.0, 0.0).astype(BF16), r.both[...])
        slot = jnp.where(hot_one, earlier[:, :LANES], earlier[:, LANES:] + firsts)
        kept = jnp.logical_and(jnp.logical_or(hot_one, hot_two), slot < limits)
        r.pos[rows, :] = jnp.where(kept, slot, -1.0)
        return carry

    lax.fori_loop(0, images, place, 0)
    r.pos_rows[...] = jnp.transpose(r.pos[...])[0 : r.pos_rows.shape[0], :]


def hits(slots, total, pos_row):
    return row_index(slots, total).astype(F32) == pos_row


def project(images, r):
    total = images * ROWS
    width = r.tokens.shape[1]
    r.triple[total:, :] = jnp.zeros((r.triple.shape[0] - total, r.triple.shape[1]), BF16)
    gain, shift = r.norms[0:1, :], r.norms[1:2, :]

    def one(i, carry):
        rows = pl.ds(pl.multiple_of(i * ROWS, 16), ROWS)
        ready = (normed(r.whole[rows, :])[0] * gain + shift).astype(BF16)
        r.first[rows, :] = ready
        r.triple[rows, :] = nn(ready, r.dense[:, r.qkv_at]).astype(BF16)
        return carry

    lax.fori_loop(0, images, one, 0)


def attend_image(i, r):
    width = r.tokens.shape[1]
    head_size = width // HEADS
    scale = head_size ** (-0.5)
    low = lane_index(1, LANES) < head_size
    real = lane_index(1, KEYS) < SEQ
    spot = lane_index(1, LANES)
    zero = jnp.zeros((), BF16)
    start = pl.multiple_of(i * ROWS, 16)
    rows = pl.ds(start, ROWS)
    keys = pl.ds(start, KEYS)
    sums = jnp.zeros((ROWS, LANES), F32)
    for pair in range(HEADS // 2):
        query_at, key_at, value_at = r.spans[pair]
        query = r.triple[rows, query_at]
        key = r.triple[keys, key_at]
        value = r.triple[keys, value_at]
        blend = jnp.zeros((ROWS, LANES), F32)
        for side in range(2):
            mine = low if side == 0 else jnp.logical_not(low)
            scores = nt(query, jnp.where(mine, key, zero)) * scale
            scores = jnp.where(real, scores, -1e30)
            top = jnp.max(scores, axis=1, keepdims=True)
            expo = jnp.exp(scores - top)
            summed = jnp.sum(expo, axis=1, keepdims=True)
            sums = jnp.where(spot == pair * 2 + side, top + jnp.log(summed), sums)
            weights = (expo * (1.0 / summed)).astype(BF16)
            blend = blend + nn(weights, jnp.where(mine, value, zero))
        r.mixed[rows, pair * LANES : (pair + 1) * LANES] = blend.astype(BF16)
    r.logsum[rows, :] = sums
    after = r.whole[rows, :] + nn(r.mixed[rows, :], r.dense[:, r.proj_at])
    r.resid[rows, :] = after
    ready = (normed(after)[0] * r.norms[2:3, :] + r.norms[3:4, :]).astype(BF16)
    r.second[rows, :] = ready
    logits = nn(ready, r.router[...])
    lane = lane_index(ROWS, LANES).astype(F32)
    choose = r.picked[rows, :]
    hot_one = lane == choose[:, 0:1]
    hot_two = lane == choose[:, 1:2]
    level_one = jnp.sum(jnp.where(hot_one, logits, 0.0), axis=1, keepdims=True)
    level_two = jnp.sum(jnp.where(hot_two, logits, 0.0), axis=1, keepdims=True)
    top = jnp.maximum(level_one, level_two)
    expo_one = jnp.exp(level_one - top)
    expo_two = jnp.exp(level_two - top)
    summed = expo_one + expo_two
    r.gates[rows, :] = jnp.where(
        hot_one, expo_one / summed, jnp.where(hot_two, expo_two / summed, 0.0)
    )


def read_tail(experts, labels, r):
    width = r.dense.shape[0]
    tail = r.dense[:, 4 * width :]
    r.norms[0:4, :] = jnp.transpose(tail.astype(F32))[experts : experts + 4, :]
    r.router[...] = nn(tail, label_matrix(experts, labels)).astype(BF16)


def gelu_pair(pre):
    half = 0.5 + 0.5 * lax.erf(pre * 0.7071067811865476)
    slope = half + pre * (jnp.exp(pre * pre * -0.5) * 0.3989422804014327)
    return pre * half, slope


def expert_block(x, da, weights, tiles, keep):
    rows, width = x.shape
    answer = jnp.zeros((rows, width), F32)
    drow = jnp.zeros((rows, width), F32)
    for j in range(tiles):
        up, down = weights(j)
        hidden, slope = gelu_pair(nn(x, up))
        hidden = hidden.astype(BF16)
        dpre = (nn(da, down) * slope).astype(BF16)
        keep(j, hidden, dpre)
        answer = answer + nt(hidden, down)
        drow = drow + nt(dpre, up)
    return answer, drow


def norm_back(grad, values, gain):
    xhat, scale = normed(values)
    dgain = jnp.sum(grad * xhat, axis=0, keepdims=True)
    dshift = jnp.sum(grad, axis=0, keepdims=True)
    inner = grad * gain
    mean_one = jnp.mean(inner, axis=1, keepdims=True)
    mean_two = jnp.mean(inner * xhat, axis=1, keepdims=True)
    return (inner - mean_one - xhat * mean_two) * scale, dgain, dshift


def router_back(i, gate, dws, drow_sum, mixing, r):
    width = r.tokens.shape[1]
    rows = pl.ds(pl.multiple_of(i * ROWS, 16), ROWS)
    dchosen = gate * (dws - jnp.sum(gate * dws, axis=1, keepdims=True))
    dlogits = nt(dchosen.astype(BF16), mixing).astype(BF16)
    r.dlogits[rows, :] = dlogits
    r.dsecond[rows, :] = drow_sum + nt(dlogits, r.dense[:, 4 * width :])


def second_norm_back(i, r):
    width = r.tokens.shape[1]
    rows = pl.ds(pl.multiple_of(i * ROWS, 16), ROWS)
    dx, dgain, dshift = norm_back(r.dsecond[rows, :], r.resid[rows, :], r.norms[2:3, :])
    dx = dx + r.dpad[rows, :].astype(F32)
    r.small[2:3, :] += dgain
    r.small[3:4, :] += dshift
    r.dres[rows, :] = dx
    dattn = dx.astype(BF16)
    r.dattn[rows, :] = dattn
    r.dmix[rows, :] = nt(dattn, r.dense[:, r.proj_at]).astype(BF16)


def attend_back(i, pair, r):
    width = r.tokens.shape[1]
    head_size = width // HEADS
    scale = head_size ** (-0.5)
    low = lane_index(1, LANES) < head_size
    real = lane_index(1, KEYS) < SEQ
    zero = jnp.zeros((), BF16)
    start = pl.multiple_of(i * ROWS, 16)
    rows = pl.ds(start, ROWS)
    keys = pl.ds(start, KEYS)
    query_at, key_at, value_at = r.spans[pair]
    sums = r.logsum[rows, :]
    query = r.triple[rows, query_at]
    key = r.triple[keys, key_at]
    value = r.triple[keys, value_at]
    dm = r.dmix[rows, pair * LANES : (pair + 1) * LANES]
    dq = jnp.zeros((ROWS, LANES), F32)
    dk = jnp.zeros((KEYS, LANES), F32)
    dv = jnp.zeros((KEYS, LANES), F32)
    for side in range(2):
        mine = low if side == 0 else jnp.logical_not(low)
        head = pair * 2 + side
        key_mine = jnp.where(mine, key, zero)
        dm_mine = jnp.where(mine, dm, zero)
        scores = nt(query, key_mine) * scale
        probs = jnp.where(real, jnp.exp(scores - sums[:, head : head + 1]), 0.0)
        dprobs = nt(dm_mine, value)
        inner = jnp.sum(dprobs * probs, axis=1, keepdims=True)
        dscores = (probs * (dprobs - inner)).astype(BF16)
        dv = dv + tn(probs.astype(BF16), dm_mine)
        dq = dq + nn(dscores, key_mine)
        dk = dk + tn(dscores, jnp.where(mine, query, zero))
    r.dtriple[rows, query_at] = (dq * scale).astype(BF16)
    r.dtriple[rows, key_at] = (dk * scale)[:ROWS].astype(BF16)
    r.dtriple[rows, value_at] = dv[:ROWS].astype(BF16)


def first_norm_back(i, r):
    width = r.tokens.shape[1]
    rows = pl.ds(pl.multiple_of(i * ROWS, 16), ROWS)
    dfirst = nt(r.dtriple[rows, :], r.dense[:, r.qkv_at])
    dx, dgain, dshift = norm_back(dfirst, r.whole[rows, :], r.norms[0:1, :])
    r.small[0:1, :] += dgain
    r.small[1:2, :] += dshift
    r.dres[rows, :] += dx


def tail_grads(experts, r):
    width = r.tokens.shape[1]
    tail = tn(r.second[...], r.dlogits[...])
    columns = jnp.transpose(
        jnp.concatenate([r.small[...], jnp.zeros((LANES - 8, width), F32)], axis=0)
    )
    shifted = pltpu.roll(columns, experts, 1)
    return jnp.where(lane_index(width, LANES) < experts, tail, shifted)


def natural_layout(width):
    return types.SimpleNamespace(
        spans=natural_spans(width), qkv_at=slice(0, 3 * width), proj_at=slice(3 * width, 4 * width)
    )


def natural_spans(width):
    return [
        tuple(slice(k * width + pair * LANES, k * width + (pair + 1) * LANES) for k in range(3))
        for pair in range(HEADS // 2)
    ]


def paired_spans():
    return [
        tuple(slice((pair * 3 + k) * LANES, (pair * 3 + k + 1) * LANES) for k in range(3))
        for pair in range(HEADS // 2)
    ]


def adam_terms(weight, grad, first, second):
    new_first = beta_one * first + (1.0 - beta_one) * grad
    new_second = beta_two * second + (1.0 - beta_two) * grad * grad
    corr_one = 1.0 - beta_one**STEP
    corr_two = 1.0 - beta_two**STEP
    update = (
        new_first / corr_one / (jnp.sqrt(new_second / corr_two) + adam_eps) + decay_rate * weight
    )
    return (new_first, new_second, update)


def take_saved(r, refs):
    (r.first, r.triple, r.logsum, r.mixed, r.resid, r.second, r.pos, r.gates) = refs


def saved_shapes(total, width):
    return (
        ((total, width), BF16),
        ((total + KEYS - ROWS, 3 * width), BF16),
        ((total, LANES), F32),
        ((total, width), BF16),
        ((total, width), F32),
        ((total, width), BF16),
        ((total, LANES), F32),
        ((total, LANES), F32),
    )


def take_route(r, refs):
    (
        r.turned, r.columns, r.picked, r.both, r.pos_rows, r.whole, r.dpad, r.wide, r.norms, r.router,
    ) = refs


def route_shapes(count, total, width, experts):
    padded = ceil_to(count, LANES)
    return (
        ((LANES, padded), F32),
        ((padded, LANES), F32),
        ((total, LANES), F32),
        ((total, 2 * LANES), BF16),
        ((ceil_to(experts, 8), total), F32),
        ((total, width), F32),
        ((total, width), BF16),
        ((ceil_to(count, 8), width), F32),
        ((8, width), F32),
        ((width, LANES), BF16),
    )


def structs(shapes):
    return tuple(jax.ShapeDtypeStruct(*one) for one in shapes)


def buffers(shapes):
    return [pltpu.VMEM(*one) for one in shapes]


def plain_attend(tokens, dout, routes, capacity, dense, slots):
    count, width = tokens.shape
    experts = capacity.shape[0]
    images = count // SEQ
    total = images * ROWS
    shape = jax.ShapeDtypeStruct

    def body(*refs):
        r = natural_layout(width)
        (r.tokens, r.dout, r.routes, r.capacity, r.dense) = refs[:5]
        take_saved(r, refs[5:13])
        r.sent, r.weight_rows = refs[13], refs[-1]
        take_route(r, refs[14:-1])
        spread_images(images, r.tokens, r.wide, r.whole)
        spread_images(images, r.dout, r.wide, r.dpad)
        read_tail(experts, None, r)
        route(images, experts, None, r)
        project(images, r)

        def image(i, carry):
            attend_image(i, r)
            return carry

        lax.fori_loop(0, images, image, 0)
        weighted = jnp.where(r.pos[...] >= 0.0, r.gates[...], 0.0)
        r.weight_rows[...] = jnp.transpose(weighted)[0 : r.weight_rows.shape[0], :]

        def dispatch(e, carry):
            hit = hits(slots, total, r.pos_rows[pl.ds(e, 1), :])
            share = jnp.sum(jnp.where(hit, r.weight_rows[pl.ds(e, 1), :], 0.0), axis=1, keepdims=True)
            place = jnp.where(hit, 1.0, 0.0).astype(BF16)
            r.sent[e, :, 0:width] = nn(place, r.second[...]).astype(BF16)
            r.sent[e, :, width:] = (nn(place, r.dpad[...]) * share).astype(BF16)
            return carry

        lax.fori_loop(0, experts, dispatch, 0)

    return pl.pallas_call(
        body,
        out_shape=structs(saved_shapes(total, width)) + (shape((experts, slots, 2 * width), BF16),),
        in_specs=[VMEM, VMEM, VMEM, SMEM, VMEM],
        out_specs=(VMEM,) * 9,
        scratch_shapes=buffers(route_shapes(count, total, width, experts))
        + [pltpu.VMEM((ceil_to(experts, 8), total), F32)],
        compiler_params=params(),
        name="attend",
    )(tokens, dout, routes, capacity, dense)


def plain_expert(arrived, up, down):
    rows = arrived.shape[0]
    width, hidden_size = up.shape
    chunk = 320
    while rows % chunk:
        chunk -= 16
    tile = 512
    shape = jax.ShapeDtypeStruct

    def body(*refs):
        r = types.SimpleNamespace()
        (r.arrived, r.up, r.down, r.back, r.grad_up, r.grad_down, r.hiddens, r.dpres) = refs

        def block(b, carry):
            at = pl.ds(pl.multiple_of(b * chunk, 16), chunk)

            def weights(j):
                cols = slice(j * tile, (j + 1) * tile)
                return r.up[:, cols], r.down[:, cols]

            def keep(j, hidden, dpre):
                r.hiddens[at, j * tile : (j + 1) * tile] = hidden
                r.dpres[at, j * tile : (j + 1) * tile] = dpre

            answer, drow = expert_block(
                r.arrived[at, 0:width], r.arrived[at, width:], weights, hidden_size // tile, keep
            )
            r.back[at, 0:width] = answer.astype(BF16)
            r.back[at, width:] = drow.astype(BF16)
            return carry

        lax.fori_loop(0, rows // chunk, block, 0)

        def grads(j, carry):
            cols = pl.ds(pl.multiple_of(j * 256, 256), 256)
            r.grad_up[:, cols] = tn(r.arrived[:, 0:width], r.dpres[:, cols])
            r.grad_down[:, cols] = tn(r.arrived[:, width:], r.hiddens[:, cols])
            return carry

        lax.fori_loop(0, hidden_size // 256, grads, 0)

    return pl.pallas_call(
        body,
        out_shape=(
            shape((rows, 2 * width), BF16),
            shape((width, hidden_size), F32),
            shape((width, hidden_size), F32),
        ),
        in_specs=[VMEM] * 3,
        out_specs=(VMEM,) * 3,
        scratch_shapes=[pltpu.VMEM((rows, hidden_size), BF16)] * 2,
        compiler_params=params(),
        name="expert",
    )(arrived, up, down)


def plain_backward(tokens, dout, dense, saved, back):
    count, width = tokens.shape
    experts, slots, _ = back.shape
    images = count // SEQ
    total = images * ROWS
    shape = jax.ShapeDtypeStruct

    def body(*refs):
        r = natural_layout(width)
        (r.tokens, r.dout, r.dense) = refs[:3]
        take_saved(r, refs[3:11])
        (r.back, r.output, r.input_grad, r.grads) = refs[11:15]
        (
            r.wide, r.whole, r.dpad, r.dlogits, r.dsecond, r.dtriple,
            r.dres, r.dattn, r.dmix, r.small, r.norms, r.router, r.outs,
        ) = refs[15:]
        spread_images(images, r.tokens, r.wide, r.whole)
        spread_images(images, r.dout, r.wide, r.dpad)
        read_tail(experts, None, r)
        mixing = label_matrix(experts, None)
        lane = lane_index(ROWS, LANES)
        slot = lane_index(ROWS, slots).astype(F32)

        def combine(i, carry):
            rows = pl.ds(pl.multiple_of(i * ROWS, 16), ROWS)
            dhere = r.dpad[rows, :].astype(F32)
            gate = r.gates[rows, :]
            spots = r.pos[rows, :]

            def one(e, sums):
                out, dws, dr = sums
                mine = lane == e
                at = jnp.sum(jnp.where(mine, spots, 0.0), axis=1, keepdims=True)
                share = jnp.sum(jnp.where(mine, gate, 0.0), axis=1, keepdims=True)
                place = jnp.where(slot == at, 1.0, 0.0).astype(BF16)
                both = nn(place, r.back[e])
                answer = both[:, 0:width]
                out = out + share * answer
                dws = jnp.where(mine, jnp.sum(dhere * answer, axis=1, keepdims=True), dws)
                return (out, dws, dr + both[:, width:])

            start = (r.resid[rows, :], jnp.zeros((ROWS, LANES), F32), jnp.zeros((ROWS, width), F32))
            out, dws, dr = lax.fori_loop(0, experts, one, start)
            r.outs[rows, :] = out
            router_back(i, gate, dws, dr, mixing, r)
            return carry

        lax.fori_loop(0, images, combine, 0)
        gather_images(images, r.outs, r.wide, r.output)
        r.small[...] = jnp.zeros_like(r.small)

        def middle(i, carry):
            second_norm_back(i, r)
            return carry

        lax.fori_loop(0, images, middle, 0)

        def image(i, carry):
            for pair in range(HEADS // 2):
                attend_back(i, pair, r)
            first_norm_back(i, r)
            return carry

        lax.fori_loop(0, images, image, 0)
        gather_images(images, r.dres, r.wide, r.input_grad)
        r.grads[:, 3 * width : 4 * width] = tn(r.mixed[...], r.dattn[...])
        r.grads[:, 4 * width :] = tail_grads(experts, r)
        for k in range(3):
            cols = slice(k * width, (k + 1) * width)
            r.grads[:, cols] = tn(r.first[...], r.dtriple[:, cols])

    return pl.pallas_call(
        body,
        out_shape=(
            shape((count, width), BF16),
            shape((count, width), BF16),
            shape((width, 4 * width + LANES), F32),
        ),
        in_specs=[VMEM] * 12,
        out_specs=(VMEM,) * 3,
        scratch_shapes=buffers(
            (
                ((ceil_to(count, 8), width), F32),
                ((total, width), F32),
                ((total, width), BF16),
                ((total, LANES), BF16),
                ((total, width), F32),
                ((total, 3 * width), BF16),
                ((total, width), F32),
                ((total, width), BF16),
                ((total, width), BF16),
                ((8, width), F32),
                ((8, width), F32),
                ((width, LANES), BF16),
                ((total, width), F32),
            )
        ),
        compiler_params=params(),
        name="backward",
    )(tokens, dout, dense, *saved, back)


def squares(values):
    return jnp.sum(values * values)


def plain_step(
    block_input, out_cotangent, route_ids, capacity,
    qkv_weight, qkv_first, qkv_second,
    proj_weight, proj_first, proj_second,
    router_weight, router_first, router_second,
    norm_params, norm_first, norm_second,
    expert_up, up_first, up_second,
    expert_down, down_first, down_second,
):
    count, width = block_input.shape
    experts = router_weight.shape[1]
    slots = ceil_to(max(2, 3 * count // lax.axis_size("expert")), 16)
    rows_dev = qkv_weight.shape[0]
    dense = jnp.concatenate(
        [qkv_weight, proj_weight, router_weight, norm_params,
         jnp.zeros((rows_dev, LANES - experts - 4), F32)], axis=1
    ).astype(BF16)
    dense = lax.all_gather(dense, "head", axis=0, tiled=True)
    up_w = lax.all_gather(expert_up[0].astype(BF16), "head", axis=1, tiled=True)
    down_w = lax.all_gather(expert_down[0].astype(BF16), "head", axis=1, tiled=True)
    *saved, sent = plain_attend(block_input, out_cotangent, route_ids.T, capacity, dense, slots)
    arrived = lax.all_to_all(sent, "expert", split_axis=0, concat_axis=0, tiled=True)
    back, grad_up, grad_down = plain_expert(arrived.reshape(experts * slots, 2 * width), up_w, down_w)
    back = lax.all_to_all(
        back.reshape(experts, slots, 2 * width), "expert", split_axis=0, concat_axis=0, tiled=True
    )
    block_output, input_grad, grads = plain_backward(block_input, out_cotangent, dense, saved, back)
    summed = lax.psum_scatter(grads, "head", scatter_dimension=0, tiled=True)
    summed = lax.psum(summed, "expert")
    shares = (
        summed[:, 0 : 3 * width],
        summed[:, 3 * width : 4 * width],
        summed[:, 4 * width : 4 * width + experts],
        summed[:, 4 * width + experts : 4 * width + experts + 4],
    )
    expert_grads = (
        lax.psum_scatter(grad_up, "head", scatter_dimension=1, tiled=True),
        lax.psum_scatter(grad_down, "head", scatter_dimension=1, tiled=True),
    )
    qkv_m, qkv_v, qkv_r = adam_terms(qkv_weight, shares[0], qkv_first, qkv_second)
    proj_m, proj_v, proj_r = adam_terms(proj_weight, shares[1], proj_first, proj_second)
    router_m, router_v, router_r = adam_terms(router_weight, shares[2], router_first, router_second)
    norm_m, norm_v, norm_r = adam_terms(norm_params, shares[3], norm_first, norm_second)
    up_m, up_v, up_r = adam_terms(expert_up, expert_grads[0][None], up_first, up_second)
    down_m, down_v, down_r = adam_terms(expert_down, expert_grads[1][None], down_first, down_second)
    weight_col = jnp.concatenate(
        [
            jnp.stack([squares(qkv_weight), squares(proj_weight), squares(router_weight)]),
            jnp.sum(norm_params * norm_params, axis=0),
        ]
    )
    update_col = jnp.concatenate(
        [
            jnp.stack([squares(qkv_r), squares(proj_r), squares(router_r)]),
            jnp.sum(norm_r * norm_r, axis=0),
        ]
    )
    expert_sq = jnp.stack(
        [squares(expert_up), squares(up_r), squares(expert_down), squares(down_r)]
    )[None, :]
    totals = lax.psum((jnp.stack([weight_col, update_col], axis=1), expert_sq), "head")
    dense_norms = jnp.sqrt(totals[0])
    expert_norms = jnp.sqrt(totals[1])
    trust = dense_norms[:, 0] / dense_norms[:, 1]
    qkv_new = qkv_weight - learn_rate * trust[0] * qkv_r
    proj_new = proj_weight - learn_rate * trust[1] * proj_r
    router_new = router_weight - learn_rate * trust[2] * router_r
    norm_new = norm_params - learn_rate * trust[3:][None, :] * norm_r
    up_new = expert_up - learn_rate * (expert_norms[0, 0] / expert_norms[0, 1]) * up_r
    down_new = expert_down - learn_rate * (expert_norms[0, 2] / expert_norms[0, 3]) * down_r
    return (
        block_output, input_grad,
        qkv_new, qkv_new.astype(BF16), qkv_m, qkv_v,
        proj_new, proj_new.astype(BF16), proj_m, proj_v,
        router_new, router_new.astype(BF16), router_m, router_v,
        norm_new, norm_new.astype(BF16), norm_m, norm_v,
        up_new, up_new.astype(BF16), up_m, up_v,
        down_new, down_new.astype(BF16), down_m, down_v,
        dense_norms, expert_norms,
    )


UNITS = 8
GROUP = 4


def arrival(ref, sem, target):
    remote(ref, ref, sem, sem, target).wait_recv()


def block(ref, i, size):
    return ref.at[pl.ds(pl.multiple_of(i * size, 8), size), :]


def total_of(values):
    return jnp.sum(jnp.sum(values * values, axis=1, keepdims=True), axis=0, keepdims=True)


def dense_order(width):
    spans = paired_spans()
    qkv = [spans[j % 3][j // 3] for j in range(9)]
    return (
        [slice(width + at.start, width + at.stop) for at in qkv]
        + [slice(j * LANES, (j + 1) * LANES) for j in range(3)]
        + [slice(4 * width, 4 * width + LANES)]
    )


def core_inputs(r, refs):
    (
        r.tokens, r.dout, r.routes, r.capacity,
        r.qkv_w, r.proj_w, r.router_w, r.norm_w, r.up_w, r.down_w,
        r.router_m, r.router_v, r.norm_m, r.norm_v,
        r.qkv_m_hbm, r.qkv_v_hbm, r.proj_m_hbm, r.proj_v_hbm,
        r.up_m_hbm, r.up_v_hbm, r.down_m_hbm, r.down_v_hbm,
    ) = refs


def core_outputs(r, refs):
    (r.output, r.input_grad, r.sum_recv, r.full, r.norm_row) = refs


def core_scratch(r, refs):
    (
        r.dense, r.ups, r.downs, r.own_up, r.own_down, r.square,
        r.rows, r.shares, r.douts, r.das, r.dsend, r.x, r.share, r.ssend, r.drows, r.dshares, r.arrived,
        r.hiddens, r.dpres, r.kept, r.given, r.side, r.sum_send,
        r.dsecond, r.dres, r.small, r.chunk, r.mine, r.head_out, r.head_in, r.quad_out, r.quad_in, r.half_out, r.half_in,
        r.tallies, r.qkv_m, r.qkv_v, r.proj_m, r.proj_v,
    ) = refs


def core_semaphores(r, refs):
    (
        r.dense_send, r.dense_recv, r.side_send, r.far_send, r.on_send, r.up_recv, r.down_recv,
        r.t_send, r.t_recv, r.x_send, r.x_recv, r.w_send, r.w_recv, r.d_send, r.d_recv, r.s_send, r.s_recv,
        r.a_send, r.a_recv, r.g_send, r.g_recv, r.f_send, r.f_recv,
        r.head_send, r.head_recv, r.quad_send, r.quad_recv, r.half_send, r.half_recv, r.full_send, r.full_recv,
        r.n_send, r.n_recv, r.load,
    ) = refs


def paired_core(tokens, dout, routes, capacity, weights, small_moments, moments, slots):
    count, width = tokens.shape
    images = count // SEQ
    total = images * ROWS
    rows_dev = weights[0].shape[0]
    piece = weights[4].shape[1]
    wide_dense = 4 * width + LANES
    chunks = [(j * width, width) for j in range(4)] + [(4 * width, 2 * LANES)]
    shots = [(0, 2 * width), (2 * width, 2 * width), (4 * width, 2 * LANES)]
    shot_chunks = [(0, 1), (2, 3), (4,)]
    wide_grads = 4 * width + 2 * LANES
    part = rows_dev // 2
    saved = saved_shapes(total, width)
    routing = route_shapes(count, total, width, UNITS)

    def body(*refs):
        r = types.SimpleNamespace(
            spans=paired_spans(), proj_at=slice(0, width), qkv_at=slice(width, 4 * width)
        )
        refs = list(refs)

        def take(n):
            taken = refs[:n]
            del refs[:n]
            return taken

        core_inputs(r, take(22))
        core_outputs(r, take(5))
        take_saved(r, take(len(saved)))
        take_route(r, take(len(routing)))
        core_scratch(r, take(39))
        core_semaphores(r, refs)
        r.dtriple = r.hiddens.at[0:total, 0 : 3 * width]
        r.dattn = r.hiddens.at[0:total, 3 * width : 4 * width]
        r.dmix = r.dpres.at[0:total, 0:width]
        r.dlogits = r.dpres.at[0:total, width : width + LANES]
        r.dws = r.picked

        me = bits()
        zh, zl, y, x, c = me
        h = x * 2 + c
        sibling, across = device(*turn(me, c=1)), device(*turn(me, x=1))
        corner = device(*turn(me, x=1, c=1))
        far = device(1 - zh, zl, y, x, zh)
        far_cores = [device(1 - zh, zl, y, x, k) for k in range(2)]
        labels = [held_expert(peer(me, i)) for i in range(UNITS)]
        targets = [device(*peer(me, i)) for i in range(UNITS)]
        quad = [turn(me, zl=m // 2, y=m % 2) for m in range(4)]
        quad_targets = [device(*there) for there in quad]
        opposite = device(*turn(me, zh=1))

        barrier = pltpu.get_barrier_semaphore()
        greeted = targets[1:] + [across, corner, opposite, device(*turn(me, zh=1, c=1))]
        for target in greeted:
            pl.semaphore_signal(barrier, inc=1, device_id=target, device_id_type=MESH)

        loads = [
            pltpu.make_async_copy(src, dst, r.load.at[k])
            for k, (src, dst) in enumerate(
                ((r.qkv_m_hbm, r.qkv_m), (r.qkv_v_hbm, r.qkv_v), (r.proj_m_hbm, r.proj_m), (r.proj_v_hbm, r.proj_v))
            )
        ]
        for copy in loads:
            copy.start()

        mine = pl.ds(pl.multiple_of(h * rows_dev, 16), rows_dev)
        order = dense_order(width)
        for j in range(9):
            r.dense[mine, order[j]] = r.qkv_w[:, j * LANES : (j + 1) * LANES].astype(BF16)
        r.dense[mine, r.proj_at] = r.proj_w[...].astype(BF16)
        r.square[...] = jnp.zeros_like(r.square)
        r.square[0:UNITS, 0:rows_dev] = r.router_w[...]
        r.square[UNITS : UNITS + 4, 0:rows_dev] = r.norm_w[...]
        r.dense[mine, 4 * width :] = jnp.transpose(r.square[...])[0:rows_dev, :].astype(BF16)
        r.own_up[...] = r.up_w[...].astype(BF16)
        r.own_down[...] = r.down_w[...].astype(BF16)
        parts = ((r.own_up, r.ups, r.up_recv), (r.own_down, r.downs, r.down_recv))

        @pl.when(c == zh)
        def _():
            for own, whole, _ in parts:
                whole[h] = own[...]

        pl.semaphore_wait(barrier, len(greeted))
        pending = []

        def start(copy):
            copy.start()
            pending.append(copy.wait_send)

        def when(condition, *calls):
            @pl.when(condition)
            def _():
                for call in calls:
                    call()

        def start_where(condition, copies):
            when(condition, *[copy.start for copy in copies])
            pending.append(lambda: when(condition, *[copy.wait_send for copy in copies]))

        def dense_rows(q):
            return r.dense.at[pl.ds(pl.multiple_of(q * rows_dev, 16), rows_dev), :]

        start(remote(dense_rows(h), dense_rows(h), r.dense_send.at[0], r.dense_recv.at[h], across))
        start(remote(dense_rows(h), dense_rows(h), r.dense_send.at[1], r.dense_recv.at[h], sibling))
        side = [
            remote(own, whole.at[h], r.side_send.at[p], recv.at[h], sibling)
            for p, (own, whole, recv) in enumerate(parts)
        ]

        start_where(c != zh, side)
        for p, (own, whole, recv) in enumerate(parts):
            start(remote(own, whole.at[h], r.far_send.at[p], recv.at[h], far))

        spread_images(images, r.tokens, r.wide, r.whole)
        spread_images(images, r.dout, r.wide, r.dpad)
        route(images, UNITS, labels, r)

        def placed(i):
            hit = hits(slots, total, r.pos_rows[i : i + 1, :])
            return hit, jnp.where(hit, 1.0, 0.0).astype(BF16)

        dout_sends = []
        for i in range(UNITS):
            filled = nn(placed(i)[1], r.dpad[...]).astype(BF16)
            if i == 0:
                r.douts[0:slots, :] = filled
            else:
                r.dsend[i * slots : (i + 1) * slots, :] = filled
                dout_sends.append(
                    remote(
                        block(r.dsend, i, slots), block(r.douts, i, slots),
                        r.t_send.at[i], r.t_recv.at[i], targets[i],
                    )
                )
                dout_sends[-1].start()

        next_q = (1 - x) * 2 + c
        arrival(dense_rows(next_q), r.dense_recv.at[next_q], across)
        start(
            remote(dense_rows(next_q), dense_rows(next_q), r.dense_send.at[2], r.dense_recv.at[next_q], sibling)
        )

        def onward(p):
            own, whole, recv = parts[p]
            return [
                remote(whole.at[x * 2 + k], whole.at[x * 2 + k], r.on_send.at[p * 2 + k], recv.at[x * 2 + k], across)
                for k in range(2)
            ]

        @pl.when(c == zh)
        def _():
            for p in range(2):
                other = x * 2 + 1 - c
                arrival(parts[p][1].at[other], parts[p][2].at[other], sibling)
                for copy in onward(p):
                    copy.start()

        pending.extend(copy.wait_send for p in range(2) for copy in onward(p))
        for q in (x * 2 + 1 - c, (1 - x) * 2 + 1 - c):
            arrival(dense_rows(q), r.dense_recv.at[q], sibling)
        read_tail(UNITS, labels, r)
        project(images, r)

        def far_arrived(p):
            for k in range(2):
                arrival(parts[p][1].at[x * 2 + k], parts[p][2].at[x * 2 + k], far)
            for copy in onward(p):
                copy.start()

        def image(i, carry):
            attend_image(i, r)

            @pl.when(jnp.logical_and(c != zh, i == images // 2))
            def _():
                far_arrived(0)

            return carry

        lax.fori_loop(0, images, image, 0)


        def out_copies(i, target):
            return (
                remote(block(r.rows, i, slots), block(r.x, i, slots), r.x_send.at[i], r.x_recv.at[i], target),
                remote(block(r.shares, i, 8), block(r.share, i, 8), r.w_send.at[i], r.w_recv.at[i], target),
            )

        def back_copies(i, target):
            return (
                remote(block(r.dsend, i, slots), block(r.drows, i, slots), r.d_send.at[i], r.d_recv.at[i], target),
                remote(block(r.ssend, i, 8), block(r.dshares, i, 8), r.s_send.at[i], r.s_recv.at[i], target),
            )

        weight_rows = jnp.transpose(jnp.where(r.pos[...] >= 0.0, r.gates[...], 0.0))
        for i in (*range(1, UNITS), 0):
            hit, place = placed(i)
            share = jnp.sum(jnp.where(hit, weight_rows[i : i + 1, :], 0.0), axis=1, keepdims=True)
            share = jnp.broadcast_to(to_row(share, width), (8, width))
            filled = nn(place, r.second[...]).astype(BF16)
            if i == 0:
                r.share[0:8, :] = share
                r.x[0:slots, :] = filled
            else:
                r.shares[i * 8 : (i + 1) * 8, :] = share
                r.rows[i * slots : (i + 1) * slots, :] = filled
                for copy in out_copies(i, targets[i]):
                    copy.start()

        @pl.when(c != zh)
        def _():
            far_arrived(1)

        for copy in dout_sends:
            copy.wait_send()


        def expert_rows(i):
            return (
                pl.ds(pl.multiple_of(i * slots, 16), slots),
                pl.ds(pl.multiple_of((i % GROUP) * slots, 16), slots),
                pl.ds(pl.multiple_of(i * 8, 8), 8),
                device(*peer(me, i)),
            )

        def ready(i):
            at, _, small, target = expert_rows(i)

            @pl.when(i > 0)
            def _():
                arrival(block(r.douts, i, slots), r.t_recv.at[i], target)
                for copy in out_copies(i, target):
                    copy.wait()

            d = r.douts[at, :].astype(F32)
            r.das[at, :] = (d * to_column(r.share[small, :][0:1, :], slots)).astype(BF16)

        def part_of(i, which):
            at, within, _, _ = expert_rows(i)

            def weights(k):
                return r.ups[which * 2 + k], r.downs[which * 2 + k]

            def keep(k, hidden, dpre):
                cols = pl.ds(pl.multiple_of((which * 2 + k) * piece, LANES), piece)
                r.hiddens[within, cols] = hidden
                r.dpres[within, cols] = dpre

            return expert_block(r.x[at, :], r.das[at, :], weights, 2, keep)

        def all_of(i):
            at, within, _, _ = expert_rows(i)

            def weights(q):
                return r.ups[q], r.downs[q]

            def keep(q, hidden, dpre):
                r.hiddens[within, q * piece : (q + 1) * piece] = hidden
                r.dpres[within, q * piece : (q + 1) * piece] = dpre

            return expert_block(r.x[at, :], r.das[at, :], weights, 4, keep)

        def done(i, answer, drow):
            at, _, small, target = expert_rows(i)
            answer = answer.astype(BF16)
            r.rows[at, :] = answer
            r.dsend[at, :] = drow.astype(BF16)
            dshare = jnp.sum(r.douts[at, :].astype(F32) * answer.astype(F32), axis=1, keepdims=True)
            r.ssend[small, :] = jnp.broadcast_to(to_row(dshare, width), (8, width))

            @pl.when(i > 0)
            def _():
                for copy in back_copies(i, target):
                    copy.start()

        def early(i, carry):
            ready(i)
            answer, drow = part_of(i, x)
            r.kept[i, 0:slots, 0:width] = answer
            r.kept[i, 0:slots, width:] = drow
            return carry

        def late(i, carry):
            answer, drow = part_of(i, 1 - x)
            done(i, answer + r.kept[i, 0:slots, 0:width], drow + r.kept[i, 0:slots, width:])
            return carry

        def one(i, carry):
            ready(i)
            answer, drow = all_of(i)
            done(i, answer, drow)
            return carry

        halves = [slice(p * piece, (p + 1) * piece) for p in range(2)]

        def over_x(p, k):
            return remote(
                r.given.at[k, :, halves[p]], r.side.at[k, :, halves[p]],
                r.g_send.at[p * 2 + k], r.g_recv.at[p * 2 + k], across,
            )

        def add_grads(g, x_of, k):
            at = pl.ds(g * GROUP * slots, GROUP * slots)
            cols = pl.ds(pl.multiple_of((x_of * 2 + k) * piece, LANES), piece)
            both = (tn(r.x[at, :], r.dpres[:, cols]), tn(r.das[at, :], r.hiddens[:, cols]))
            q = x_of * 2 + k
            if g == 0:
                for p in range(2):
                    r.kept[q, :, halves[p]] = both[p]
            elif x_of is x:
                for p in range(2):
                    r.kept[q, :, halves[p]] += both[p]
            else:
                for p in range(2):
                    r.given[k, :, halves[p]] = (r.kept[q, :, halves[p]] + both[p]).astype(BF16)
                    start(over_x(p, k))

        other_x = 1 - x
        for g in range(UNITS // GROUP):
            if g == 0:
                for p in range(2):
                    for k in range(2):
                        q = other_x * 2 + k
                        arrival(parts[p][1].at[q], parts[p][2].at[q], across)
            lax.fori_loop(g * GROUP, (g + 1) * GROUP, one, 0)
            for x_of in (other_x, x):
                for k in range(2):
                    add_grads(g, x_of, k)
        pending.extend(copy.wait_send for i in range(1, UNITS) for copy in back_copies(i, targets[i]))


        r.arrived[0:slots, :] = r.rows[0:slots, :]
        r.drows[0:slots, :] = r.dsend[0:slots, :]
        r.dshares[0:8, :] = r.ssend[0:8, :]
        lane = lane_index(ROWS, LANES)
        slot = lane_index(ROWS, slots).astype(F32)

        for i in range(1, UNITS):
            for copy in back_copies(i, targets[i]):
                copy.wait_recv()

        def combine(i, carry):
            rows = pl.ds(pl.multiple_of(i * ROWS, 16), ROWS)
            spots = r.pos[rows, :]
            dws = jnp.zeros((ROWS, LANES), F32)
            dr = jnp.zeros((ROWS, width), F32)
            for e in range(UNITS):
                hit = slot == spots[:, e : e + 1]
                found = jnp.where(hit, r.dshares[e * 8 : e * 8 + 1, 0:slots], 0.0)
                dws = jnp.where(lane == e, jnp.sum(found, axis=1, keepdims=True), dws)
                place = jnp.where(hit, 1.0, 0.0).astype(BF16)
                dr = dr + nn(place, r.drows[e * slots : (e + 1) * slots, :])
            r.dws[rows, :] = dws
            r.dsecond[rows, :] = dr
            return carry

        for i in range(1, UNITS):
            start(
                remote(
                    block(r.rows, i, slots), block(r.arrived, i, slots),
                    r.a_send.at[i], r.a_recv.at[i], targets[i],
                )
            )

        lax.fori_loop(0, images, combine, 0)


        def sums(p, k, target, at):
            return remote(
                r.sum_send.at[k, :, halves[p]], r.sum_recv.at[at, :, halves[p]],
                r.f_send.at[p * 2 + k], r.f_recv.at[p * 2 + at], target,
            )

        def after_x(k):
            for p in range(2):
                over_x(p, k).wait_recv()
                there = r.kept[x * 2 + k, :, halves[p]] + r.side[k, :, halves[p]].astype(F32)
                r.sum_send[k, :, halves[p]] = there.astype(BF16)
                start_where(jnp.logical_and(c == zh, c != k), [sums(p, k, sibling, 0)])
                start_where(c != zh, [sums(p, k, far_cores[k], 1)])

            @pl.when(jnp.logical_and(c == zh, c == k))
            def _():
                r.sum_recv[0] = r.sum_send[k]

        after_x(0)


        mixing = label_matrix(UNITS, labels)
        r.small[...] = jnp.zeros_like(r.small)

        def middle(i, carry):
            rows = pl.ds(pl.multiple_of(i * ROWS, 16), ROWS)
            router_back(i, r.gates[rows, :], r.dws[rows, :], r.dsecond[rows, :], mixing, r)
            second_norm_back(i, r)
            return carry

        lax.fori_loop(0, images, middle, 0)


        relations = (sibling, across, corner)
        related = (x * 2 + 1 - c, (1 - x) * 2 + c, (1 - x) * 2 + 1 - c)

        def head_copy(j, k):
            at, size = chunks[j]
            cols = slice(at, at + size)
            return remote(
                r.head_out.at[k, :, cols], r.head_in.at[k, :, cols],
                r.head_send.at[j * 3 + k], r.head_recv.at[j * 3 + k], relations[k],
            )

        def over_head(j, grads):
            at, size = chunks[j]
            cols = slice(at, at + size)
            r.chunk[:, 0:size] = grads
            for k in range(3):
                rows = pl.ds(pl.multiple_of(related[k] * rows_dev, 16), rows_dev)
                r.head_out[k, :, cols] = r.chunk[rows, 0:size].astype(BF16)
                start(head_copy(j, k))
            r.mine[:, cols] = r.chunk[mine, 0:size]

        def quarter(s, there):
            at, size = shots[s]
            rows = pl.ds(pl.multiple_of(there[2] * part, 16), part)
            return rows, pl.ds(pl.multiple_of(at + there[1] * (size // 2), LANES), size // 2)

        def first_of(s):
            at, size = shots[s]
            return slice(at // 2, (at + size) // 2)

        def quad_copy(s, m):
            return remote(
                r.quad_out.at[*quarter(s, quad[m])], r.quad_in.at[m, :, first_of(s)],
                r.quad_send.at[s * 4 + m], r.quad_recv.at[s * 4 + m], quad_targets[m],
            )

        def over_quad(s):
            for j in shot_chunks[s]:
                at, size = chunks[j]
                cols = slice(at, at + size)
                summed = r.mine[:, cols]
                for k in range(3):
                    head_copy(j, k).wait_recv()
                    summed = summed + r.head_in[k, :, cols].astype(F32)
                r.mine[:, cols] = summed
                r.quad_out[:, cols] = summed.astype(BF16)
            for m in (2, 3, 1):
                start(quad_copy(s, m))

        def half_copy(s):
            cols = first_of(s)
            return remote(
                r.half_out.at[:, cols], r.half_in.at[:, cols], r.half_send.at[s], r.half_recv.at[s], opposite
            )

        def over_halves(s):
            summed = r.mine[*quarter(s, me)]
            for m in range(1, 4):
                quad_copy(s, m).wait_recv()
                summed = summed + r.quad_in[m, :, first_of(s)].astype(F32)
            r.half_out[:, first_of(s)] = summed.astype(BF16)
            start(half_copy(s))

        def full_copy(s, m):
            there = r.full.at[*quarter(s, me)]
            return remote(
                there, there, r.full_send.at[s * 4 + m], r.full_recv.at[s * 4 + m], quad_targets[m]
            )

        def to_quad(s):
            half_copy(s).wait_recv()
            cols = first_of(s)
            summed = r.half_out[:, cols].astype(F32) + r.half_in[:, cols].astype(F32)
            r.full[*quarter(s, me)] = summed.astype(BF16)
            for m in (2, 3, 1):
                start(full_copy(s, m))

        def full_here(s):
            for m in range(1, 4):
                arrival(r.full.at[*quarter(s, quad[m])], r.full_recv.at[s * 4 + m], quad_targets[m])

        def back_pair(pair):
            def image_back(i, carry):
                attend_back(i, pair, r)
                return carry

            lax.fori_loop(0, images, image_back, 0)
            over_head(1 + pair, tn(r.first[...], r.dtriple[:, pair * width : (pair + 1) * width]))

        over_head(0, tn(r.mixed[...], r.dattn[...]))
        back_pair(0)
        back_pair(1)
        after_x(1)
        back_pair(2)
        over_quad(0)
        moment_loads = [
            pltpu.make_async_copy(src, r.kept.at[k, :, 0:piece], r.load.at[4 + k])
            for k, src in enumerate((r.up_m_hbm, r.up_v_hbm, r.down_m_hbm, r.down_v_hbm))
        ]
        for copy in moment_loads:
            copy.start()

        def first_back(i, carry):
            first_norm_back(i, r)
            return carry

        lax.fori_loop(0, images, first_back, 0)
        over_head(4, jnp.concatenate([tail_grads(UNITS, r), jnp.zeros((width, LANES), F32)], axis=1))
        over_quad(1)
        over_halves(0)
        gather_images(images, r.dres, r.wide, r.input_grad)
        over_quad(2)
        over_halves(1)

        for i in range(1, UNITS):
            arrival(block(r.arrived, i, slots), r.a_recv.at[i], targets[i])

        def combine_out(i, carry):
            rows = pl.ds(pl.multiple_of(i * ROWS, 16), ROWS)
            out = r.resid[rows, :]
            spots = r.pos[rows, :]
            gate = r.gates[rows, :]
            for e in range(UNITS):
                at = spots[:, e : e + 1]
                share = jnp.where(at >= 0.0, gate[:, e : e + 1], 0.0)
                place = jnp.where(slot == at, 1.0, 0.0).astype(BF16)
                out = out + share * nn(place, r.arrived[e * slots : (e + 1) * slots, :])
            r.dsecond[rows, :] = out
            return carry

        lax.fori_loop(0, images, combine_out, 0)
        over_halves(2)
        to_quad(0)
        to_quad(1)
        gather_images(images, r.dsecond, r.wide, r.output)
        to_quad(2)

        weights_sq, steps_sq, tally = [], [], []

        def count_in(weight, grad, first, second):
            step = adam_terms(weight, grad, first, second)[2]
            return total_of(weight), total_of(step)

        for copy in moment_loads:
            copy.wait()
        for p, weight in enumerate((r.up_w, r.down_w)):

            @pl.when(c != zh)
            def _(p=p):
                arrival(r.sum_recv.at[0, :, halves[p]], r.f_recv.at[p * 2], sibling)

            arrival(r.sum_recv.at[1, :, halves[p]], r.f_recv.at[p * 2 + 1], sibling)
            grad = r.sum_recv[0, :, halves[p]].astype(F32) + r.sum_recv[1, :, halves[p]].astype(F32)
            tally += count_in(weight[...], grad, r.kept[2 * p, :, 0:piece], r.kept[2 * p + 1, :, 0:piece])
        for copy in loads:
            copy.wait()

        def dense_grad(j):
            return r.full[:, order[j]].astype(F32)

        full_here(0)
        full_here(1)
        for weight, first, second, blocks_of in (
            (r.qkv_w, r.qkv_m, r.qkv_v, range(9)),
            (r.proj_w, r.proj_m, r.proj_v, range(9, 12)),
        ):
            sums_of = [jnp.zeros((1, 1), F32), jnp.zeros((1, 1), F32)]
            for n, j in enumerate(blocks_of):
                cols = slice(n * LANES, (n + 1) * LANES)
                both = count_in(weight[:, cols], dense_grad(j), first[:, cols], second[:, cols])
                sums_of = [a + b for a, b in zip(sums_of, both, strict=True)]
            weights_sq.append(sums_of[0])
            steps_sq.append(sums_of[1])
        full_here(2)
        r.square[...] = jnp.zeros_like(r.square)
        r.square[0:rows_dev, :] = dense_grad(12)
        turned = jnp.transpose(r.square[...])
        both = count_in(r.router_w[...], turned[0:UNITS, 0:rows_dev], r.router_m[...], r.router_v[...])
        weights_sq.append(both[0])
        steps_sq.append(both[1])
        step = adam_terms(r.norm_w[...], turned[UNITS : UNITS + 4, 0:rows_dev], r.norm_m[...], r.norm_v[...])[2]
        for k in range(4):
            weights_sq.append(total_of(r.norm_w[k : k + 1, :]))
            steps_sq.append(total_of(step[k : k + 1, :]))
        spot = lane_index(1, LANES)
        row = jnp.zeros((1, LANES), F32)
        for k, value in enumerate(weights_sq + steps_sq + tally):
            row = jnp.where(spot == k, value, row)
        r.tallies[pl.ds(pl.multiple_of(h * 8, 8), 8), :] = jnp.broadcast_to(row, (8, LANES))
        for k, target in enumerate(relations):
            start(
                remote(block(r.tallies, h, 8), block(r.tallies, h, 8), r.n_send.at[k], r.n_recv.at[h], target)
            )
        for q, target in zip(related, relations, strict=True):
            arrival(block(r.tallies, q, 8), r.n_recv.at[q], target)
        summed = r.tallies[0:8, :]
        for q in range(1, 4):
            summed = summed + r.tallies[q * 8 : (q + 1) * 8, :]
        r.norm_row[...] = jnp.sqrt(summed)

        for wait in pending:
            wait()

    dma = pltpu.SemaphoreType.DMA
    scratch = (
        ((width, wide_dense), BF16),
        ((4, width, piece), BF16),
        ((4, width, piece), BF16),
        ((width, piece), BF16),
        ((width, piece), BF16),
        ((LANES, LANES), F32),
        ((UNITS * slots, width), BF16),
        ((UNITS * 8, width), F32),
        ((UNITS * slots, width), BF16),
        ((UNITS * slots, width), BF16),
        ((UNITS * slots, width), BF16),
        ((UNITS * slots, width), BF16),
        ((UNITS * 8, width), F32),
        ((UNITS * 8, width), F32),
        ((UNITS * slots, width), BF16),
        ((UNITS * 8, width), F32),
        ((UNITS * slots, width), BF16),
        ((GROUP * slots, 4 * piece), BF16),
        ((GROUP * slots, 4 * piece), BF16),
        ((4, width, 2 * piece), F32),
        ((2, width, 2 * piece), BF16),
        ((2, width, 2 * piece), BF16),
        ((2, width, 2 * piece), BF16),
        ((total, width), F32),
        ((total, width), F32),
        ((8, width), F32),
        ((width, width), F32),
        ((rows_dev, wide_grads), F32),
        ((3, rows_dev, wide_grads), BF16),
        ((3, rows_dev, wide_grads), BF16),
        ((rows_dev, wide_grads), BF16),
        ((4, part, wide_grads // 2), BF16),
        ((part, wide_grads // 2), BF16),
        ((part, wide_grads // 2), BF16),
        ((4 * 8, LANES), F32),
        ((rows_dev, 3 * width), F32),
        ((rows_dev, 3 * width), F32),
        ((rows_dev, width), F32),
        ((rows_dev, width), F32),
    )
    semaphores = (
        [dma((n,)) for n in (3, 4, 2, 2, 4, 4, 4)]
        + [dma((UNITS,))] * 12
        + [dma((4,))] * 4
        + [dma((15,))] * 2
        + [dma((12,))] * 2
        + [dma((3,))] * 2
        + [dma((12,))] * 2
        + [dma((4,)), dma((4,)), dma((8,))]
    )
    anywhere = pl.BlockSpec(memory_space=pl.ANY)
    return pl.pallas_call(
        body,
        out_shape=structs(
            (
                ((count, width), BF16),
                ((count, width), BF16),
                ((2, width, 2 * piece), BF16),
                ((rows_dev, wide_grads), BF16),
                ((8, LANES), F32),
            )
        ),
        in_specs=[VMEM] * 3 + [SMEM] + [VMEM] * 10 + [anywhere] * 8,
        out_specs=(VMEM,) * 5,
        scratch_shapes=buffers(saved) + buffers(routing) + buffers(scratch) + semaphores,
        compiler_params=params(mib=62, collective_id=1, has_side_effects=True),
        name="core",
    )(tokens, dout, routes, capacity, *weights, *small_moments, *moments)


def paired_finish(output, input_grad, expert_sums, full, norm_row, state):
    rows_dev = state[0].shape[0]
    width, piece = state[12].shape

    def body(*refs):
        (made, made_grad, sums, dense, norms) = refs[:5]
        state_refs, outs = refs[5:23], refs[23:]
        outs[0][...] = made[...]
        outs[1][...] = made_grad[...]
        order = dense_order(width)
        row = norms[0:1, :]
        square = jnp.concatenate(
            [dense[:, order[12]].astype(F32), jnp.zeros((LANES - rows_dev, LANES), F32)], axis=0
        )
        turned = jnp.transpose(square)

        def trust(over, under):
            return learn_rate * (row[:, over : over + 1] / row[:, under : under + 1])

        def update(which, grad, scale, cols=slice(None)):
            weight, first, second = [ref[:, cols] for ref in state_refs[3 * which : 3 * which + 3]]
            new, copy, first_new, second_new = outs[2 + 4 * which : 6 + 4 * which]
            first_here, second_here, step = adam_terms(weight, grad, first, second)
            first_new[:, cols] = first_here
            second_new[:, cols] = second_here
            value = weight - scale * step
            new[:, cols] = value
            copy[:, cols] = value.astype(BF16)

        for which, at, over in ((0, 0, 0), (1, 9, 1)):
            for n in range(9 if which == 0 else 3):
                cols = slice(n * LANES, (n + 1) * LANES)
                update(which, dense[:, order[at + n]].astype(F32), trust(over, over + 7), cols)
        update(2, turned[0:UNITS, 0:rows_dev], trust(2, 9))
        scales = jnp.concatenate([trust(3 + k, 10 + k) for k in range(4)], axis=0)
        update(3, turned[UNITS : UNITS + 4, 0:rows_dev], scales)
        for p in range(2):
            cols = slice(p * piece, (p + 1) * piece)
            grad = sums[0, :, cols].astype(F32) + sums[1, :, cols].astype(F32)
            update(4 + p, grad, trust(14 + 2 * p, 15 + 2 * p))
        dense_norms, expert_norms = outs[26:]
        dense_norms[0:1, :] = row[:, 0:7]
        dense_norms[1:2, :] = pltpu.roll(row, LANES - 7, 1)[:, 0:7]
        expert_norms[...] = pltpu.roll(row, LANES - 14, 1)[:, 0:4]

    results = []
    for k in range(0, len(state), 3):
        size = state[k].shape
        results += [(size, F32), (size, BF16), (size, F32), (size, F32)]
    return pl.pallas_call(
        body,
        out_shape=structs(
            [(output.shape, BF16), (input_grad.shape, BF16)] + results + [((2, 7), F32), ((1, 4), F32)]
        ),
        in_specs=[VMEM] * 23,
        out_specs=(VMEM,) * 28,
        compiler_params=params(),
        name="finish",
    )(output, input_grad, expert_sums, full, norm_row, *state)


def paired_step(
    block_input, out_cotangent, route_ids, capacity,
    qkv_weight, qkv_first, qkv_second,
    proj_weight, proj_first, proj_second,
    router_weight, router_first, router_second,
    norm_params, norm_first, norm_second,
    expert_up, up_first, up_second,
    expert_down, down_first, down_second,
):
    count = block_input.shape[0]
    slots = ceil_to(max(2, 3 * count // lax.axis_size("expert")), 16)
    state = (
        qkv_weight, qkv_first, qkv_second,
        proj_weight, proj_first, proj_second,
        router_weight.T, router_first.T, router_second.T,
        norm_params.T, norm_first.T, norm_second.T,
        expert_up[0], up_first[0], up_second[0],
        expert_down[0], down_first[0], down_second[0],
    )
    made = paired_core(
        block_input, out_cotangent, route_ids.T, capacity,
        state[0::3], (state[7], state[8], state[10], state[11]),
        (state[1], state[2], state[4], state[5], state[13], state[14], state[16], state[17]), slots,
    )
    block_output, input_grad, *results, dense_norms, expert_norms = paired_finish(*made, state)
    for k in range(8, 16):
        results[k] = results[k].T
    for k in range(16, 24):
        results[k] = results[k][None]
    return (block_output, input_grad, *results, dense_norms.T, expert_norms)


def solution(mesh):
    tokens, dense, pair = P(("expert", "head"), None), P("head", None), P("expert", None, "head")
    small = mesh.shape["expert"] == 8 and mesh.shape["head"] == 4
    return jax.shard_map(
        paired_step if small else plain_step,
        mesh=mesh,
        in_specs=(tokens,) * 3 + (P(),) + (dense,) * 12 + (pair,) * 6,
        out_specs=(tokens,) * 2 + (dense,) * 16 + (pair,) * 8 + (P(), P("expert", None)),
        check_vma=False,
    )
```
